128 devices in a mesh: row: 8 (over x, core), col: 16 (over y, z).
Axes of the slice: x: 4, y: 4, z: 4, core: 2. Of those that a mesh axis runs over, the one named last changes fastest.
Arguments:
- theta: bfloat16 [8192, 4, 4, 2048], P('row', None, None, 'col'), may hold values from -6 to 6
- gate: bfloat16 [4, 4, 4, 4], replicated, may hold values from -1.5 to 1.5
- warm_start: bfloat16 [16, 4, 2048, 512], P('row', None, 'col'), may hold values from -0.0625 to 0.0625
- slot_sector: int32 [16], replicated, may hold values from 0 to 15, each once
- kept: int32 [16], replicated, may hold values from 128 to 512
- block_offsets: int32 [8, 16], replicated, may hold values from 0 to 992, as said below
Outputs:
- left_factor: float32 [768, 16, 4, 512], P('col', 'row')
- right_factor: float32 [16, 4, 2048, 512], P('row', None, 'col')
The draws below stay inside these ranges and needn't reach their ends.
Inputs may be any that keep to these rules, and one draw needn't show every extreme that they name: `block_offsets`: each device's block lists the sectors in order; every sector has 32 to 96 states in every block, both ends reached; offsets start at 0 and the counts of a block add up to 1024.
All inputs are finite; a program needn't handle non-finite values.
Results may differ from the reference program's by a relative error of at most 0.0042.
Values may be sent and summed in bfloat16 or wider, within the bound.
A program may use at most 512 MiB of HBM per device.

```python
import jax
import jax.numpy as jnp
from jax import lax

MEANC = 64
SPG = 2
CB = 2048
KMAX = 512
NSEC = 16
ROW_DEV = 1024
ROWS = 8192
NMAX = 96
SRC = 768


def draw_block_offsets(key, part):
    groups = NSEC // SPG
    pairs = NSEC // 2
    key_order, key_base, key_jitter = jax.random.split(jax.random.fold_in(key, 11), 3)
    order = jax.random.permutation(key_order, NSEC)
    base = jax.random.randint(key_base, (pairs,), 0, MEANC * 3 // 8 + 1)
    base = jnp.where(jnp.arange(pairs) == 0, MEANC // 2, base)
    jitter = jax.random.randint(key_jitter, (groups, pairs), 0, MEANC // 8 + 1)
    extra = jnp.minimum(base[None, :] + jitter, MEANC // 2)
    by_place = jnp.stack([MEANC + extra, MEANC - extra], axis=-1).reshape(groups, NSEC)
    inverse = jnp.argsort(order)
    counts = by_place[:, inverse]
    offsets = jnp.cumsum(counts, axis=1) - counts
    return offsets.astype(jnp.int32)


def place_ends(entries, rng, smallest, largest):
    longest = entries.shape.index(max(entries.shape))
    spots = []
    for shift in (0, 1):
        where = [jax.random.randint(jax.random.fold_in(rng, axis), (), 0, length) for axis, length in enumerate(entries.shape)]
        where[longest] = (where[longest] + shift) % entries.shape[longest]
        spots.append(tuple(where))
    return entries.at[spots[0]].set(smallest).at[spots[1]].set(largest)


def level_of(key, shape, cuts, low, high):
    factor_of, own = 1.0, jax.random.fold_in(key, 6)
    for axis_at, parts in cuts:
        steps = jnp.exp(jax.random.uniform(jax.random.fold_in(own, axis_at), (parts,), jnp.float32, low / len(cuts), high / len(cuts)))
        factor_of = factor_of * jnp.repeat(steps, shape[axis_at] // parts).reshape([-1 if axis == axis_at else 1 for axis in range(len(shape))])
    return factor_of


def gaussian(own_key, dims, spread, limit, cuts=(), held_as=jnp.bfloat16):
    drawn = spread * jax.random.normal(own_key, dims, jnp.float32)
    if cuts:
        drawn = drawn * level_of(own_key, dims, cuts, -0.22, 0.18)
    return jnp.clip(drawn, -limit, limit).astype(held_as)


def setup_inputs(seed: int = 0) -> dict:
    key_of = jax.random.split(jax.random.key(seed), 7)
    return {
        "theta": gaussian(key_of[0], (ROWS, 4, 4, CB), 1.0, 6.0, ((0, 8), (3, 16))),
        "gate": gaussian(key_of[1], (4, 4, 4, 4), 16 ** -0.5, 1.5),
        "warm_start": gaussian(key_of[2], (NSEC, 4, CB, KMAX), (4 * CB) ** -0.5, 0.0625, ((0, 8), (2, 16))),
        "slot_sector": jax.random.permutation(key_of[3], NSEC).astype(jnp.int32),
        "kept": place_ends(jax.random.randint(key_of[4], (NSEC,), KMAX // 4, KMAX + 1), jax.random.fold_in(key_of[4], 1), KMAX // 4, KMAX).astype(jnp.int32),
        "block_offsets": draw_block_offsets(jax.random.fold_in(key_of[6], 71), 0),
    }


damping = 0.25


def refine_step(gram_matrix, correlation, kept_rank):
    identity = jnp.eye(KMAX, dtype=jnp.float32)
    lambdas = jnp.diagonal(gram_matrix) / (jnp.diagonal(correlation) + 1e-6)
    resid = identity - correlation
    differ = lambdas[None, :] - lambdas[:, None]
    divisor = differ * differ + (damping * (lambdas[:, None] + lambdas[None, :])) ** 2 + 1e-6
    offdiag = (gram_matrix + lambdas[None, :] * resid) * differ / divisor
    indices = jnp.arange(KMAX)
    inside = (indices[:, None] < kept_rank) & (indices[None, :] < kept_rank)
    result = jnp.where(identity > 0.5, 0.5 * resid, offdiag)
    return jnp.where(inside, result, jnp.float32(0.0))


def reference(theta, gate, warm_start, slot_sector, kept, block_offsets):
    groups = NSEC // SPG
    closing = jnp.full((groups, 1), ROW_DEV, jnp.int32)
    counts = jnp.concatenate([block_offsets[:, 1:], closing], axis=1) - block_offsets
    places = jnp.arange(NMAX, dtype=jnp.int32)

    def one_slot(slot):
        sector = slot_sector[slot]
        starts = block_offsets[:, sector]
        amounts = counts[:, sector]
        row_index = jnp.minimum(starts[:, None] + places[None, :], ROW_DEV - 1)
        global_rows = (jnp.arange(groups, dtype=jnp.int32)[:, None] * ROW_DEV + row_index).reshape(-1)
        live_mask = (places[None, :] < amounts[:, None]).reshape(-1)
        picked = theta[global_rows]
        gated = jnp.einsum('abef,refc->rabc', gate.astype(jnp.float32), picked.astype(jnp.float32))
        gated = jnp.where(live_mask[:, None, None, None], gated, jnp.float32(0.0)).astype(jnp.bfloat16)
        a_rows = gated.reshape(SRC, 4, 4 * CB)
        vectors = warm_start[slot].reshape(4 * CB, KMAX)
        projected = jnp.einsum('rtn,nk->rtk', a_rows.astype(jnp.float32), vectors.astype(jnp.float32))
        correlation = jnp.dot(vectors.T, vectors, preferred_element_type=jnp.float32)
        projected_b = projected.astype(jnp.bfloat16)
        flattened = projected_b.reshape(SRC * 4, KMAX)
        gram_matrix = jnp.dot(flattened.T, flattened, preferred_element_type=jnp.float32)
        kept_rank = kept[sector]
        corr_b = refine_step(gram_matrix, correlation, kept_rank).astype(jnp.bfloat16)
        kept_mask = (jnp.arange(KMAX) < kept_rank).astype(jnp.float32)
        new_vectors = (vectors.astype(jnp.float32) + jnp.dot(vectors, corr_b, preferred_element_type=jnp.float32)) * kept_mask[None, :]
        left = projected + jnp.einsum('rtk,kl->rtl', projected_b.astype(jnp.float32), corr_b.astype(jnp.float32))
        left = left * kept_mask[None, None, :]
        return left, new_vectors.reshape(4, CB, KMAX)

    lefts, rights = lax.map(one_slot, jnp.arange(NSEC, dtype=jnp.int32))
    return jnp.transpose(lefts, (1, 0, 2, 3)), rights
```

```python
import jax
import jax.numpy as jnp
from jax import lax
from jax.sharding import PartitionSpec as P

NMAX = 96


damping = 0.25


def refine_step(gram_matrix, correlation, gram_diag, corr_diag, kept_rank):
    kept_most = gram_matrix.shape[0]
    identity = jnp.eye(kept_most, dtype=jnp.float32)
    lambdas = gram_diag / (corr_diag + 1e-06)
    resid = identity - correlation
    differ = lambdas[None, :] - lambdas[:, None]
    divisor = differ * differ + (damping * (lambdas[:, None] + lambdas[None, :])) ** 2 + 1e-06
    offdiag = (gram_matrix + lambdas[None, :] * resid) * differ / divisor
    indices = jnp.arange(kept_most)
    inside = (indices[:, None] < kept_rank) & (indices[None, :] < kept_rank)
    result = jnp.where(identity > 0.5, 0.5 * resid, offdiag)
    return jnp.where(inside, result, jnp.float32(0.0))


def shards(theta, gate, warm_start, slot_sector, kept, block_offsets):
    row_devices = lax.axis_size("row")
    my_row = lax.axis_index("row")
    block_rows = theta.shape[0]
    bond_cols = theta.shape[3]
    sectors = slot_sector.shape[0]
    per_group = sectors // row_devices
    kept_most = warm_start.shape[3]
    gated = jnp.einsum("abef,refc->rabc", gate, theta, preferred_element_type=jnp.float32)
    gated = gated.astype(jnp.bfloat16).reshape(block_rows, 4, 4 * bond_cols)
    closing = jnp.full((row_devices, 1), block_rows, jnp.int32)
    counts = jnp.concatenate([block_offsets[:, 1:], closing], axis=1) - block_offsets
    mine_start = lax.dynamic_index_in_dim(block_offsets, my_row, 0, keepdims=False)
    mine_count = lax.dynamic_index_in_dim(counts, my_row, 0, keepdims=False)
    sector_ids = jnp.arange(sectors, dtype=jnp.int32)
    chooser = (slot_sector[:, None] == sector_ids[None, :]).astype(jnp.int32)
    slot_start = jnp.sum(chooser * mine_start[None, :], axis=1)
    slot_count = jnp.sum(chooser * mine_count[None, :], axis=1)
    places = jnp.arange(NMAX, dtype=jnp.int32)
    row_index = jnp.minimum(slot_start[None, :] + places[:, None], block_rows - 1)
    live_mask = places[:, None] < slot_count[None, :]
    outgoing = jnp.where(live_mask[:, :, None, None], gated[row_index], jnp.zeros((), jnp.bfloat16))
    blocks = lax.all_to_all(outgoing, "row", split_axis=1, concat_axis=0, tiled=True)
    vectors = warm_start.reshape(per_group, 4 * bond_cols, kept_most)
    my_sectors = lax.dynamic_slice_in_dim(slot_sector, my_row * per_group, per_group, 0)
    my_chooser = (my_sectors[:, None] == sector_ids[None, :]).astype(jnp.int32)
    my_kept = jnp.sum(my_chooser * kept[None, :], axis=1)
    correlation_part = jnp.einsum(
        "snk,snl->skl", vectors, vectors, preferred_element_type=jnp.float32
    )
    correlation = lax.psum(correlation_part, "col")
    identity = jnp.eye(kept_most, dtype=jnp.float32)[None]
    projected = lax.psum_scatter(
        jnp.einsum("istn,snk->istk", blocks, vectors, preferred_element_type=jnp.float32),
        "col",
        scatter_dimension=0,
        tiled=True,
    )
    projected_b = projected.astype(jnp.bfloat16)
    gram_part = jnp.einsum(
        "istk,istl->skl", projected_b, projected_b, preferred_element_type=jnp.float32
    )
    gram_matrix = lax.psum(gram_part, "col")
    gram_diag = jnp.sum(gram_matrix * identity, axis=1)
    corr_diag = jnp.sum(correlation * identity, axis=1)
    corr_b = jax.vmap(refine_step)(gram_matrix, correlation, gram_diag, corr_diag, my_kept).astype(jnp.bfloat16)
    kept_mask = (jnp.arange(kept_most)[None, :] < my_kept[:, None]).astype(jnp.float32)
    new_vectors = vectors.astype(jnp.float32) + jnp.einsum(
        "snk,skl->snl", vectors, corr_b, preferred_element_type=jnp.float32
    )
    new_vectors = new_vectors * kept_mask[:, None, :]
    left = projected + jnp.einsum(
        "istk,skl->istl", projected_b, corr_b, preferred_element_type=jnp.float32
    )
    left = left * kept_mask[None, :, None, :]
    return (left, new_vectors.reshape(per_group, 4, bond_cols, kept_most))


def solution(mesh):
    in_specs = (P("row", None, None, "col"), P(), P("row", None, "col", None), P(), P(), P())
    out_specs = (P("col", "row", None, None), P("row", None, "col", None))
    return jax.shard_map(shards, mesh=mesh, in_specs=in_specs, out_specs=out_specs, check_vma=False)
```

```python
import functools

import jax
import jax.numpy as jnp
from jax import lax
from jax.experimental import pallas as pl
from jax.experimental.pallas import tpu as pltpu
from jax.sharding import PartitionSpec as P

NMAX = 96
HALF = NMAX // 2
SITES = 4
LANES = 128
KEPT = 512
ROWS = 1024
DAMPING = 0.25
MESH = pl.DeviceIdType.MESH

ORDER = (
    (0, 0), (0, 1), (1, 0), (1, 1),
    (2, 0), (3, 0), (4, 0), (5, 0),
    (2, 1), (3, 1), (4, 1), (5, 1),
    (6, 0), (6, 1), (7, 0), (7, 1),
)
UNITS = len(ORDER)
LAG = (2, 4, 6)


def project_kernel(
    theta_ref, gate_ref, v_ref, sector_ref, offset_ref, fin_ref,
    th, bd, ap, vall, part, half_in, ring_in, quart, quart_in, done,
    th_sem, v_sem, v_send, v_recv, half_send, half_recv, ring_send, ring_recv,
    quart_send, quart_recv, fin_send, fin_recv,
):
    row, col = lax.axis_index("row"), lax.axis_index("col")
    x, core = row // 2, row % 2
    y, z = col // 4, col % 4
    other = 1 - core

    def rows_at(step, which):
        return ((x + step) % 4) * 2 + which

    places = (
        row, rows_at(0, other), rows_at(3, core), rows_at(1, core),
        rows_at(3, other), rows_at(1, other), rows_at(2, core), rows_at(2, other),
    )
    sibling, before, after = places[1], places[2], places[3]

    def along(axis, step):
        if axis == 0:
            return {"row": row, "col": y * 4 + (z + step) % 4}
        return {"row": row, "col": ((y + step) % 4) * 4 + z}

    sends = []

    def send(src, dst, send_sem, recv_sem, where):
        copy = pltpu.make_async_remote_copy(
            src_ref=src, dst_ref=dst, send_sem=send_sem, recv_sem=recv_sem,
            device_id=where, device_id_type=MESH,
        )
        copy.start()
        sends.append(copy)

    def arrived(dst, sem):
        pltpu.make_async_copy(dst, dst, sem).wait()

    theta_in = pltpu.make_async_copy(theta_ref, th.at[pl.ds(0, ROWS)], th_sem)
    theta_in.start()
    v_in = pltpu.make_async_copy(v_ref, vall.at[0], v_sem)
    v_in.start()
    for s in range(2):
        for n, (where, place) in enumerate(((sibling, 1), (after, 2), (before, 3))):
            send(v_ref.at[s], vall.at[place, s], v_send.at[3 * s + n], v_recv.at[place, s], {"row": where, "col": col})

    big_r = lax.broadcasted_iota(jnp.int32, (256, 256), 0)
    big_c = lax.broadcasted_iota(jnp.int32, (256, 256), 1)
    left_hot = (lax.broadcasted_iota(jnp.int32, (256, 16), 0) // 16 == lax.broadcasted_iota(jnp.int32, (256, 16), 1))
    right_hot = (lax.broadcasted_iota(jnp.int32, (16, 256), 1) % 16 == lax.broadcasted_iota(jnp.int32, (16, 256), 0))
    spread = jnp.dot(left_hot.astype(jnp.bfloat16), gate_ref[...], preferred_element_type=jnp.float32)
    spread = jnp.dot(spread.astype(jnp.bfloat16), right_hot.astype(jnp.bfloat16), preferred_element_type=jnp.float32)
    bd[...] = jnp.where(big_r % 16 == big_c // 16, spread, 0.0).astype(jnp.bfloat16)
    th[pl.ds(ROWS, NMAX)] = jnp.zeros((NMAX, 16, LANES), jnp.bfloat16)
    theta_in.wait()
    v_in.wait()

    state = lax.broadcasted_iota(jnp.int32, (256, 256), 0) % 16
    state = state + 16 * (lax.broadcasted_iota(jnp.int32, (256, 256), 1) // LANES)

    def compute(u):
        place, s = ORDER[u]
        slot = places[place] * 2 + s
        if place:
            arrived(vall.at[place, s], v_recv.at[place, s])
            if place in (2, 3, 6):
                share = {2: 4, 3: 5, 6: 7}[place]
                if place == 2 and s == 0:
                    send(vall.at[2, 0], vall.at[6, 0], v_send.at[6], v_recv.at[6, 0], {"row": after, "col": col})
                if place == 3 and s == 1:
                    send(vall.at[3, 1], vall.at[6, 1], v_send.at[7], v_recv.at[6, 1], {"row": before, "col": col})
                n = 8 + 2 * (2, 3, 6).index(place) + s
                send(vall.at[place, s], vall.at[share, s], v_send.at[n], v_recv.at[share, s], {"row": sibling, "col": col})
        sector = sector_ref[slot]
        start = offset_ref[row, sector]
        end = jnp.where(sector == 15, ROWS, offset_ref[row, jnp.minimum(sector + 1, 15)])
        count = end - start
        for k in range(0, NMAX // 16, 2):
            both = th[pl.ds(start + 16 * k, 32)].reshape(512, LANES)
            both = jnp.concatenate([both[:256], both[256:]], axis=1)
            gated = jnp.dot(bd[...], both, preferred_element_type=jnp.float32)
            gated = jnp.where(state + 16 * k < count, gated, 0.0).astype(jnp.bfloat16)
            for a in range(SITES):
                for b in range(SITES):
                    for m in range(2):
                        ap[a * NMAX + 16 * (k + m): a * NMAX + 16 * (k + m + 1), b * LANES:(b + 1) * LANES] = gated[
                            (a * 4 + b) * 16:(a * 4 + b + 1) * 16, m * LANES:(m + 1) * LANES]
        product = jnp.dot(ap[...], vall[place, s], preferred_element_type=jnp.float32).astype(jnp.bfloat16)
        for a in range(SITES):
            part[u, a] = product[a * NMAX:(a + 1) * NMAX]
        axis = u % 2
        mine = z if axis == 0 else y
        far = (mine + 2) % 4
        send(part.at[u, far, pl.ds(0, HALF)], half_in.at[u, 0], half_send.at[u, 0], half_recv.at[u, 0], along(axis, 1))
        send(part.at[u, far, pl.ds(HALF, HALF)], half_in.at[u, 1], half_send.at[u, 1], half_recv.at[u, 1], along(axis, 3))

    def pass_on(u):
        axis = u % 2
        mine = z if axis == 0 else y
        for n, step in ((0, 1), (1, 3)):
            arrived(half_in.at[u, n], half_recv.at[u, n])
            to = (mine + step) % 4
            rows = pl.ds(n * HALF, HALF)
            total = part[u, to, rows, :].astype(jnp.float32) + half_in[u, n].astype(jnp.float32)
            part[u, to, rows, :] = total.astype(jnp.bfloat16)
            send(part.at[u, to], ring_in.at[u, n], ring_send.at[u, n], ring_recv.at[u, n], along(axis, step))

    def split(u):
        axis = u % 2
        mine = z if axis == 0 else y
        second = y if axis == 0 else z
        for n in range(2):
            arrived(ring_in.at[u, n], ring_recv.at[u, n])
        total = part[u, mine].astype(jnp.float32) + ring_in[u, 0].astype(jnp.float32) + ring_in[u, 1].astype(jnp.float32)
        total = total.astype(jnp.bfloat16)
        for q in range(4):
            quart[u, q] = total[:, q * LANES:(q + 1) * LANES]
        for d in (2, 1, 3):
            send(quart.at[u, (second + d) % 4], quart_in.at[u, d - 1], quart_send.at[u, d - 1],
                 quart_recv.at[u, d - 1], along(1 - axis, d))

    def finish(u):
        axis = u % 2
        place, s = ORDER[u]
        mine = z if axis == 0 else y
        second = y if axis == 0 else z
        total = quart[u, second].astype(jnp.float32)
        for d in (1, 2, 3):
            arrived(quart_in.at[u, d - 1], quart_recv.at[u, d - 1])
            total = total + quart_in[u, d - 1].astype(jnp.float32)
        done[u] = total.astype(jnp.bfloat16)
        for h in range(2):
            src = done.at[u, pl.ds(h * HALF, HALF)]
            dst = fin_ref.at[s, mine, second]
            target = 2 * row + h
            if place == 0:
                @pl.when(col == target)
                def _():
                    pltpu.make_async_copy(src, dst, fin_recv.at[s, col]).start()

                @pl.when(col != target)
                def _():
                    pltpu.make_async_remote_copy(
                        src_ref=src, dst_ref=dst, send_sem=fin_send.at[u, h], recv_sem=fin_recv.at[s, col],
                        device_id={"row": places[place], "col": target}, device_id_type=MESH).start()
            else:
                send(src, dst, fin_send.at[u, h], fin_recv.at[s, col], {"row": places[place], "col": target})

    for step in range(UNITS + LAG[2]):
        if step < UNITS:
            compute(step)
        if 0 <= step - LAG[0] < UNITS:
            pass_on(step - LAG[0])
        if 0 <= step - LAG[1] < UNITS:
            split(step - LAG[1])
        if 0 <= step - LAG[2] < UNITS:
            finish(step - LAG[2])

    for s in range(2):
        @pl.loop(0, 16)
        def _(c):
            arrived(fin_ref.at[s, 0, 0], fin_recv.at[s, c])

    for copy in sends:
        copy.wait_send()
    for s in range(2):
        for h in range(2):
            @pl.when(col != 2 * row + h)
            def _():
                pltpu.make_async_copy(done.at[s, pl.ds(h * HALF, HALF)], done.at[s, pl.ds(h * HALF, HALF)], fin_send.at[s, h]).wait()


def project(theta, gate, vectors, slot_sector, block_offsets):
    bf = jnp.bfloat16
    dma = pltpu.SemaphoreType.DMA
    vmem = pl.BlockSpec(memory_space=pltpu.VMEM)
    smem = pl.BlockSpec(memory_space=pltpu.SMEM)
    hbm = pl.BlockSpec(memory_space=pl.ANY)
    return pl.pallas_call(
        project_kernel,
        out_shape=jax.ShapeDtypeStruct((2, SITES, 4, HALF, LANES), bf),
        in_specs=[hbm, vmem, hbm, smem, smem],
        out_specs=vmem,
        scratch_shapes=[
            pltpu.VMEM((ROWS + NMAX, 16, LANES), bf),
            pltpu.VMEM((256, 256), bf),
            pltpu.VMEM((SITES * NMAX, KEPT), bf),
            pltpu.VMEM((8, 2, KEPT, KEPT), bf),
            pltpu.VMEM((UNITS, SITES, NMAX, KEPT), bf),
            pltpu.VMEM((UNITS, 2, HALF, KEPT), bf),
            pltpu.VMEM((UNITS, 2, NMAX, KEPT), bf),
            pltpu.VMEM((UNITS, 4, NMAX, LANES), bf),
            pltpu.VMEM((UNITS, 3, NMAX, LANES), bf),
            pltpu.VMEM((UNITS, NMAX, LANES), bf),
            dma, dma, dma((14,)), dma((8, 2)),
            dma((UNITS, 2)), dma((UNITS, 2)), dma((UNITS, 2)), dma((UNITS, 2)),
            dma((UNITS, 3)), dma((UNITS, 3)), dma((UNITS, 2)), dma((2, 16)),
        ],
        compiler_params=pltpu.CompilerParams(has_side_effects=True, vmem_limit_bytes=56 * 2**20),
        cost_estimate=pl.CostEstimate(flops=5_000_000_000, bytes_accessed=6_000_000, transcendentals=0),
        name="project",
    )(theta, gate, vectors, slot_sector, block_offsets)


def refine_step(gram_matrix, correlation, gram_diag, corr_diag, kept_rank):
    kept_most = gram_matrix.shape[0]
    identity = jnp.eye(kept_most, dtype=jnp.float32)
    lambdas = gram_diag / (corr_diag + 1e-06)
    resid = identity - correlation
    differ = lambdas[None, :] - lambdas[:, None]
    divisor = differ * differ + (DAMPING * (lambdas[:, None] + lambdas[None, :])) ** 2 + 1e-06
    offdiag = (gram_matrix + lambdas[None, :] * resid) * differ / divisor
    indices = jnp.arange(kept_most)
    inside = (indices[:, None] < kept_rank) & (indices[None, :] < kept_rank)
    result = jnp.where(identity > 0.5, 0.5 * resid, offdiag)
    return jnp.where(inside, result, jnp.float32(0.0))


def shards(theta, gate, warm_start, slot_sector, kept, block_offsets):
    my_row = lax.axis_index("row")
    vectors = warm_start.reshape(2, KEPT, KEPT)
    fin = project(theta.reshape(ROWS, 16, LANES), gate.reshape(16, 16), vectors, slot_sector, block_offsets)
    projected_b = fin.transpose(0, 1, 3, 2, 4).reshape(2, SITES * HALF, KEPT)
    correlation_part = jnp.einsum("snk,snl->skl", vectors, vectors, preferred_element_type=jnp.float32)
    gram_part = jnp.einsum("snk,snl->skl", projected_b, projected_b, preferred_element_type=jnp.float32)
    correlation = lax.psum(correlation_part, "col")
    gram_matrix = lax.psum(gram_part, "col")
    my_sectors = lax.dynamic_slice_in_dim(slot_sector, my_row * 2, 2, 0)
    my_chooser = (my_sectors[:, None] == jnp.arange(16, dtype=jnp.int32)[None, :]).astype(jnp.int32)
    my_kept = jnp.sum(my_chooser * kept[None, :], axis=1)
    identity = jnp.eye(KEPT, dtype=jnp.float32)[None]
    gram_diag = jnp.sum(gram_matrix * identity, axis=1)
    corr_diag = jnp.sum(correlation * identity, axis=1)
    corr_b = jax.vmap(refine_step)(gram_matrix, correlation, gram_diag, corr_diag, my_kept).astype(jnp.bfloat16)
    kept_mask = (jnp.arange(KEPT)[None, :] < my_kept[:, None]).astype(jnp.float32)
    new_vectors = vectors.astype(jnp.float32) + jnp.einsum(
        "snk,skl->snl", vectors, corr_b, preferred_element_type=jnp.float32
    )
    new_vectors = new_vectors * kept_mask[:, None, :]
    left = projected_b.astype(jnp.float32) + jnp.einsum(
        "snk,skl->snl", projected_b, corr_b, preferred_element_type=jnp.float32
    )
    left = left * kept_mask[:, None, :]
    left = left.reshape(2, SITES, HALF, KEPT).transpose(2, 0, 1, 3)
    return (left, new_vectors.reshape(2, 4, LANES, KEPT))


def solution(mesh):
    in_specs = (P("row", None, None, "col"), P(), P("row", None, "col", None), P(), P(), P())
    out_specs = (P("col", "row", None, None), P("row", None, "col", None))
    return jax.shard_map(shards, mesh=mesh, in_specs=in_specs, out_specs=out_specs, check_vma=False)
```

```python
import jax
import jax.numpy as jnp
from jax import lax
from jax.experimental import pallas as pl
from jax.experimental.pallas import tpu as pltpu
from jax.sharding import PartitionSpec as P

NMAX = 96
HALF = NMAX // 2
SITES = 4
LANES = 128
SHARE = 32
KEPT = 512
ROWS = 1024
DAMPING = 0.25
MESH = pl.DeviceIdType.MESH

ORDER = (
    (0, 0), (0, 1), (1, 0), (1, 1),
    (2, 0), (3, 0), (4, 0), (5, 0),
    (2, 1), (3, 1), (4, 1), (5, 1),
    (6, 0), (6, 1), (7, 0), (7, 1),
)
UNITS = len(ORDER)
LAG = (2, 4, 6)


def overlap(factor, out, diag, row, col):
    for s in range(2):
        block = factor[s]
        product = lax.dot_general(block, block, (((0,), (0,)), ((), ())), preferred_element_type=jnp.float32)
        product = product.astype(jnp.bfloat16)
        for c in range(16):
            out[c, s] = product[c * SHARE:(c + 1) * SHARE]
        wide = block.astype(jnp.float32)
        squares = jnp.sum(wide * wide, axis=0, keepdims=True)
        for q in range(4):
            diag[col, s * 4 + q:s * 4 + q + 1] = squares[:, q * LANES:(q + 1) * LANES]


def start_exchange(out, into, send_sem, recv_sem, row, col):
    @pl.loop(1, 16)
    def _(d):
        to = (col + d) % 16
        pltpu.make_async_remote_copy(
            src_ref=out.at[to], dst_ref=into.at[col], send_sem=send_sem.at[to], recv_sem=recv_sem.at[col],
            device_id={"row": row, "col": to}, device_id_type=MESH).start()


def start_shared(both, send_sem, recv_sem, row, col):
    @pl.loop(1, 16)
    def _(d):
        to = (col + d) % 16
        pltpu.make_async_remote_copy(
            src_ref=both.at[col], dst_ref=both.at[col], send_sem=send_sem.at[to], recv_sem=recv_sem.at[col],
            device_id={"row": row, "col": to}, device_id_type=MESH).start()


def wait_on(ref, sem):
    pltpu.make_async_copy(ref, ref, sem).wait()


def finish_exchange(out, into, send_sem, recv_sem, col):
    @pl.loop(1, 16)
    def _(d):
        source = (col + d) % 16
        wait_on(into.at[source], recv_sem.at[source])
        wait_on(out.at[source], send_sem.at[source])

    into[col] = out[col]
    total = into[0].astype(jnp.float32)
    for c in range(1, 16):
        total = total + into[c].astype(jnp.float32)
    return total


def finish_shared(both, send_sem, recv_sem, col):
    @pl.loop(1, 16)
    def _(d):
        source = (col + d) % 16
        wait_on(both.at[source], recv_sem.at[source])
        wait_on(both.at[col], send_sem.at[source])

    return jnp.sum(both[...], axis=0)


def refine_kernel(
    fin_ref, corr_ref, corr_diag_ref, sector_ref, kept_ref, out_ref, mask_ref,
    factor, gram_out, gram_in, diag_in, gram_send, gram_recv, diag_send, diag_recv, out_send, out_recv,
):
    row, col = lax.axis_index("row"), lax.axis_index("col")
    barrier = pltpu.get_barrier_semaphore()

    @pl.loop(1, 16)
    def _(d):
        pl.semaphore_signal(barrier, inc=1, device_id={"row": row, "col": (col + d) % 16}, device_id_type=MESH)

    for s in range(2):
        for a in range(SITES):
            for q in range(4):
                factor[s, a * HALF:(a + 1) * HALF, q * LANES:(q + 1) * LANES] = fin_ref[s, a, q]
    overlap(factor, gram_out, diag_in, row, col)
    pl.semaphore_wait(barrier, 15)
    start_shared(diag_in, diag_send, diag_recv, row, col)
    start_exchange(gram_out, gram_in, gram_send, gram_recv, row, col)
    gram_diag = finish_shared(diag_in, diag_send, diag_recv, col)
    corr_diag = corr_diag_ref[...]
    lambdas = gram_diag / (corr_diag + 1e-06)
    gram = finish_exchange(gram_out, gram_in, gram_send, gram_recv, col)
    at_row = lax.broadcasted_iota(jnp.int32, (SHARE, KEPT), 0) + SHARE * col
    at_col = lax.broadcasted_iota(jnp.int32, (SHARE, KEPT), 1)
    for s in range(2):
        kept = kept_ref[sector_ref[2 * row + s]]
        across = jnp.concatenate([lambdas[s * 4 + q:s * 4 + q + 1] for q in range(4)], axis=1)
        norms = jnp.concatenate([corr_diag[s * 4 + q:s * 4 + q + 1] for q in range(4)], axis=1)
        across = jnp.broadcast_to(across, (SHARE, KEPT))
        down = jnp.sum(jnp.where(at_row == at_col, across, 0.0), axis=1, keepdims=True)
        differ = across - down
        mean = DAMPING * (across + down)
        divisor = differ * differ + mean * mean + 1e-06
        offdiag = (gram[s] - across * corr_ref[s]) * differ / divisor
        result = jnp.where(at_row == at_col, 0.5 * (1.0 - norms), offdiag)
        result = jnp.where((at_row < kept) & (at_col < kept), result, 0.0)
        out_ref[s, col] = result.astype(jnp.bfloat16)
        lanes = lax.broadcasted_iota(jnp.int32, (8, KEPT), 1)
        mask_ref[s] = jnp.where(lanes < kept, 1.0, 0.0)

    @pl.loop(1, 16)
    def _(d):
        to = (col + d) % 16
        pltpu.make_async_remote_copy(
            src_ref=out_ref.at[:, col], dst_ref=out_ref.at[:, col], send_sem=out_send.at[to],
            recv_sem=out_recv.at[col], device_id={"row": row, "col": to}, device_id_type=MESH).start()

    @pl.loop(1, 16)
    def _(d):
        source = (col + d) % 16
        wait_on(out_ref.at[:, source], out_recv.at[source])
        wait_on(out_ref.at[:, col], out_send.at[source])


def refine(fin, correlation, corr_diag, slot_sector, kept):
    bf = jnp.bfloat16
    dma = pltpu.SemaphoreType.DMA
    vmem = pl.BlockSpec(memory_space=pltpu.VMEM)
    smem = pl.BlockSpec(memory_space=pltpu.SMEM)
    return pl.pallas_call(
        refine_kernel,
        out_shape=(jax.ShapeDtypeStruct((2, 16, SHARE, KEPT), bf), jax.ShapeDtypeStruct((2, 8, KEPT), jnp.float32)),
        in_specs=[vmem, vmem, vmem, smem, smem],
        out_specs=(vmem, vmem),
        scratch_shapes=[
            pltpu.VMEM((2, SITES * HALF, KEPT), bf),
            pltpu.VMEM((16, 2, SHARE, KEPT), bf),
            pltpu.VMEM((16, 2, SHARE, KEPT), bf),
            pltpu.VMEM((16, 8, LANES), jnp.float32),
        ] + [dma((16,))] * 6,
        compiler_params=pltpu.CompilerParams(has_side_effects=True, collective_id=1, vmem_limit_bytes=32 * 2**20),
        cost_estimate=pl.CostEstimate(flops=200_000_000, bytes_accessed=2_000_000, transcendentals=0),
        name="refine",
    )(fin, correlation, corr_diag, slot_sector, kept)


def project_kernel(
    theta_ref, gate_ref, v_ref, sector_ref, offset_ref, fin_ref, corr_ref, corr_diag_ref,
    corr_out, corr_in, diag_in, th, bd, ap, vall, part, half_in, ring_in, quart, quart_in, done,
    th_sem, v_sem, v_send, v_recv, half_send, half_recv, ring_send, ring_recv,
    quart_send, quart_recv, fin_send, fin_recv, corr_send, corr_recv, diag_send, diag_recv,
):
    row, col = lax.axis_index("row"), lax.axis_index("col")
    x, core = row // 2, row % 2
    y, z = col // 4, col % 4
    other = 1 - core

    def rows_at(step, which):
        return ((x + step) % 4) * 2 + which

    places = (
        row, rows_at(0, other), rows_at(3, core), rows_at(1, core),
        rows_at(3, other), rows_at(1, other), rows_at(2, core), rows_at(2, other),
    )
    sibling, before, after = places[1], places[2], places[3]

    def along(axis, step):
        if axis == 0:
            return {"row": row, "col": y * 4 + (z + step) % 4}
        return {"row": row, "col": ((y + step) % 4) * 4 + z}

    sends = []

    def send(src, dst, send_sem, recv_sem, where):
        copy = pltpu.make_async_remote_copy(
            src_ref=src, dst_ref=dst, send_sem=send_sem, recv_sem=recv_sem,
            device_id=where, device_id_type=MESH,
        )
        copy.start()
        sends.append(copy)

    def arrived(dst, sem):
        pltpu.make_async_copy(dst, dst, sem).wait()

    theta_in = pltpu.make_async_copy(theta_ref, th.at[pl.ds(0, ROWS)], th_sem)
    theta_in.start()
    v_in = pltpu.make_async_copy(v_ref, vall.at[0], v_sem)
    v_in.start()
    for s in range(2):
        for n, (where, place) in enumerate(((sibling, 1), (after, 2), (before, 3))):
            send(v_ref.at[s], vall.at[place, s], v_send.at[3 * s + n], v_recv.at[place, s], {"row": where, "col": col})

    big_r = lax.broadcasted_iota(jnp.int32, (256, 256), 0)
    big_c = lax.broadcasted_iota(jnp.int32, (256, 256), 1)
    left_hot = (lax.broadcasted_iota(jnp.int32, (256, 16), 0) // 16 == lax.broadcasted_iota(jnp.int32, (256, 16), 1))
    right_hot = (lax.broadcasted_iota(jnp.int32, (16, 256), 1) % 16 == lax.broadcasted_iota(jnp.int32, (16, 256), 0))
    spread = jnp.dot(left_hot.astype(jnp.bfloat16), gate_ref[...], preferred_element_type=jnp.float32)
    spread = jnp.dot(spread.astype(jnp.bfloat16), right_hot.astype(jnp.bfloat16), preferred_element_type=jnp.float32)
    bd[...] = jnp.where(big_r % 16 == big_c // 16, spread, 0.0).astype(jnp.bfloat16)
    th[pl.ds(ROWS, NMAX)] = jnp.zeros((NMAX, 16, LANES), jnp.bfloat16)
    theta_in.wait()
    v_in.wait()

    state = lax.broadcasted_iota(jnp.int32, (256, 256), 0) % 16
    state = state + 16 * (lax.broadcasted_iota(jnp.int32, (256, 256), 1) // LANES)

    def compute(u):
        place, s = ORDER[u]
        slot = places[place] * 2 + s
        if place:
            arrived(vall.at[place, s], v_recv.at[place, s])
            if place in (2, 3, 6):
                share = {2: 4, 3: 5, 6: 7}[place]
                if place == 2 and s == 0:
                    send(vall.at[2, 0], vall.at[6, 0], v_send.at[6], v_recv.at[6, 0], {"row": after, "col": col})
                if place == 3 and s == 1:
                    send(vall.at[3, 1], vall.at[6, 1], v_send.at[7], v_recv.at[6, 1], {"row": before, "col": col})
                n = 8 + 2 * (2, 3, 6).index(place) + s
                send(vall.at[place, s], vall.at[share, s], v_send.at[n], v_recv.at[share, s], {"row": sibling, "col": col})
        sector = sector_ref[slot]
        start = offset_ref[row, sector]
        end = jnp.where(sector == 15, ROWS, offset_ref[row, jnp.minimum(sector + 1, 15)])
        count = end - start
        for k in range(0, NMAX // 16, 2):
            both = th[pl.ds(start + 16 * k, 32)].reshape(512, LANES)
            both = jnp.concatenate([both[:256], both[256:]], axis=1)
            gated = jnp.dot(bd[...], both, preferred_element_type=jnp.float32)
            gated = jnp.where(state + 16 * k < count, gated, 0.0).astype(jnp.bfloat16)
            for a in range(SITES):
                for b in range(SITES):
                    for m in range(2):
                        ap[a * NMAX + 16 * (k + m): a * NMAX + 16 * (k + m + 1), b * LANES:(b + 1) * LANES] = gated[
                            (a * 4 + b) * 16:(a * 4 + b + 1) * 16, m * LANES:(m + 1) * LANES]
        product = jnp.dot(ap[...], vall[place, s], preferred_element_type=jnp.float32).astype(jnp.bfloat16)
        for a in range(SITES):
            part[u, a] = product[a * NMAX:(a + 1) * NMAX]
        axis = u % 2
        mine = z if axis == 0 else y
        far = (mine + 2) % 4
        send(part.at[u, far, pl.ds(0, HALF)], half_in.at[u, 0], half_send.at[u, 0], half_recv.at[u, 0], along(axis, 1))
        send(part.at[u, far, pl.ds(HALF, HALF)], half_in.at[u, 1], half_send.at[u, 1], half_recv.at[u, 1], along(axis, 3))

    def pass_on(u):
        axis = u % 2
        mine = z if axis == 0 else y
        for n, step in ((0, 1), (1, 3)):
            arrived(half_in.at[u, n], half_recv.at[u, n])
            to = (mine + step) % 4
            rows = pl.ds(n * HALF, HALF)
            total = part[u, to, rows, :].astype(jnp.float32) + half_in[u, n].astype(jnp.float32)
            part[u, to, rows, :] = total.astype(jnp.bfloat16)
            send(part.at[u, to], ring_in.at[u, n], ring_send.at[u, n], ring_recv.at[u, n], along(axis, step))

    def split(u):
        axis = u % 2
        mine = z if axis == 0 else y
        second = y if axis == 0 else z
        for n in range(2):
            arrived(ring_in.at[u, n], ring_recv.at[u, n])
        total = part[u, mine].astype(jnp.float32) + ring_in[u, 0].astype(jnp.float32) + ring_in[u, 1].astype(jnp.float32)
        total = total.astype(jnp.bfloat16)
        for q in range(4):
            quart[u, q] = total[:, q * LANES:(q + 1) * LANES]
        for d in (2, 1, 3):
            send(quart.at[u, (second + d) % 4], quart_in.at[u, d - 1], quart_send.at[u, d - 1],
                 quart_recv.at[u, d - 1], along(1 - axis, d))

    def finish(u):
        axis = u % 2
        place, s = ORDER[u]
        mine = z if axis == 0 else y
        second = y if axis == 0 else z
        total = quart[u, second].astype(jnp.float32)
        for d in (1, 2, 3):
            arrived(quart_in.at[u, d - 1], quart_recv.at[u, d - 1])
            total = total + quart_in[u, d - 1].astype(jnp.float32)
        done[u] = total.astype(jnp.bfloat16)
        for h in range(2):
            src = done.at[u, pl.ds(h * HALF, HALF)]
            dst = fin_ref.at[s, mine, second]
            target = 2 * row + h
            if place == 0:
                @pl.when(col == target)
                def _():
                    pltpu.make_async_copy(src, dst, fin_recv.at[s, col]).start()

                @pl.when(col != target)
                def _():
                    pltpu.make_async_remote_copy(
                        src_ref=src, dst_ref=dst, send_sem=fin_send.at[u, h], recv_sem=fin_recv.at[s, col],
                        device_id={"row": places[place], "col": target}, device_id_type=MESH).start()
            else:
                send(src, dst, fin_send.at[u, h], fin_recv.at[s, col], {"row": places[place], "col": target})

    for step in range(UNITS + LAG[2]):
        if step < UNITS:
            compute(step)
        if step == 3:
            overlap(vall.at[0], corr_out, diag_in, row, col)
            start_exchange(corr_out, corr_in, corr_send, corr_recv, row, col)
            start_shared(diag_in, diag_send, diag_recv, row, col)
        if 0 <= step - LAG[0] < UNITS:
            pass_on(step - LAG[0])
        if 0 <= step - LAG[1] < UNITS:
            split(step - LAG[1])
        if 0 <= step - LAG[2] < UNITS:
            finish(step - LAG[2])

    corr_ref[...] = finish_exchange(corr_out, corr_in, corr_send, corr_recv, col)
    corr_diag_ref[...] = finish_shared(diag_in, diag_send, diag_recv, col)

    for s in range(2):
        @pl.loop(0, 16)
        def _(c):
            arrived(fin_ref.at[s, 0, 0], fin_recv.at[s, c])

    for copy in sends:
        copy.wait_send()
    for s in range(2):
        for h in range(2):
            @pl.when(col != 2 * row + h)
            def _():
                pltpu.make_async_copy(done.at[s, pl.ds(h * HALF, HALF)], done.at[s, pl.ds(h * HALF, HALF)], fin_send.at[s, h]).wait()


def project(theta, gate, vectors, slot_sector, block_offsets):
    bf = jnp.bfloat16
    dma = pltpu.SemaphoreType.DMA
    vmem = pl.BlockSpec(memory_space=pltpu.VMEM)
    smem = pl.BlockSpec(memory_space=pltpu.SMEM)
    hbm = pl.BlockSpec(memory_space=pl.ANY)
    return pl.pallas_call(
        project_kernel,
        out_shape=(
            jax.ShapeDtypeStruct((2, SITES, 4, HALF, LANES), bf),
            jax.ShapeDtypeStruct((2, SHARE, KEPT), jnp.float32),
            jax.ShapeDtypeStruct((8, LANES), jnp.float32),
        ),
        in_specs=[hbm, vmem, hbm, smem, smem],
        out_specs=(vmem, vmem, vmem),
        scratch_shapes=[
            pltpu.VMEM((16, 2, SHARE, KEPT), bf),
            pltpu.VMEM((16, 2, SHARE, KEPT), bf),
            pltpu.VMEM((16, 8, LANES), jnp.float32),
            pltpu.VMEM((ROWS + NMAX, 16, LANES), bf),
            pltpu.VMEM((256, 256), bf),
            pltpu.VMEM((SITES * NMAX, KEPT), bf),
            pltpu.VMEM((8, 2, KEPT, KEPT), bf),
            pltpu.VMEM((UNITS, SITES, NMAX, KEPT), bf),
            pltpu.VMEM((UNITS, 2, HALF, KEPT), bf),
            pltpu.VMEM((UNITS, 2, NMAX, KEPT), bf),
            pltpu.VMEM((UNITS, 4, NMAX, LANES), bf),
            pltpu.VMEM((UNITS, 3, NMAX, LANES), bf),
            pltpu.VMEM((UNITS, NMAX, LANES), bf),
            dma, dma, dma((14,)), dma((8, 2)),
            dma((UNITS, 2)), dma((UNITS, 2)), dma((UNITS, 2)), dma((UNITS, 2)),
            dma((UNITS, 3)), dma((UNITS, 3)), dma((UNITS, 2)), dma((2, 16)),
            dma((16,)), dma((16,)), dma((16,)), dma((16,)),
        ],
        compiler_params=pltpu.CompilerParams(has_side_effects=True, vmem_limit_bytes=56 * 2**20),
        cost_estimate=pl.CostEstimate(flops=5_000_000_000, bytes_accessed=6_000_000, transcendentals=0),
        name="project",
    )(theta, gate, vectors, slot_sector, block_offsets)


def shards(theta, gate, warm_start, slot_sector, kept, block_offsets):
    vectors = warm_start.reshape(2, KEPT, KEPT)
    fin, correlation, corr_diag = project(theta.reshape(ROWS, 16, LANES), gate.reshape(16, 16), vectors, slot_sector, block_offsets)
    corr_b, mask = refine(fin, correlation, corr_diag, slot_sector, kept)
    corr_b = corr_b.reshape(2, KEPT, KEPT)
    kept_mask = mask[:, 0]
    projected_b = fin.transpose(0, 1, 3, 2, 4).reshape(2, SITES * HALF, KEPT)
    new_vectors = vectors.astype(jnp.float32) + jnp.einsum(
        "snk,skl->snl", vectors, corr_b, preferred_element_type=jnp.float32
    )
    new_vectors = new_vectors * kept_mask[:, None, :]
    left = projected_b.astype(jnp.float32) + jnp.einsum(
        "snk,skl->snl", projected_b, corr_b, preferred_element_type=jnp.float32
    )
    left = left * kept_mask[:, None, :]
    left = left.reshape(2, SITES, HALF, KEPT).transpose(2, 0, 1, 3)
    return (left, new_vectors.reshape(2, 4, LANES, KEPT))


def solution(mesh):
    in_specs = (P("row", None, None, "col"), P(), P("row", None, "col", None), P(), P(), P())
    out_specs = (P("col", "row", None, None), P("row", None, "col", None))
    return jax.shard_map(shards, mesh=mesh, in_specs=in_specs, out_specs=out_specs, check_vma=False)
```

```python
import jax
import jax.numpy as jnp
from jax import lax
from jax.experimental import pallas as pl
from jax.experimental.pallas import tpu as pltpu
from jax.sharding import PartitionSpec as P

NMAX = 96
HALF = NMAX // 2
SITES = 4
LANES = 128
SHARE = 32
KEPT = 512
ROWS = 1024
DAMPING = 0.25
MESH = pl.DeviceIdType.MESH

ORDER = (
    (0, 0), (0, 1), (1, 0), (1, 1),
    (2, 0), (3, 0), (4, 0), (5, 0),
    (2, 1), (3, 1), (4, 1), (5, 1),
    (6, 0), (6, 1), (7, 0), (7, 1),
)
UNITS = len(ORDER)


def overlap(factor, out, diag, row, col):
    for s in range(2):
        block = factor[s]
        product = lax.dot_general(block, block, (((0,), (0,)), ((), ())), preferred_element_type=jnp.float32)
        product = product.astype(jnp.bfloat16)
        for c in range(16):
            out[c, s] = product[c * SHARE:(c + 1) * SHARE]
        wide = block.astype(jnp.float32)
        squares = jnp.sum(wide * wide, axis=0, keepdims=True)
        for q in range(4):
            diag[col, s * 4 + q:s * 4 + q + 1] = squares[:, q * LANES:(q + 1) * LANES]


def start_exchange(out, into, send_sem, recv_sem, row, col):
    @pl.loop(1, 16)
    def _(d):
        to = (col + d) % 16
        pltpu.make_async_remote_copy(
            src_ref=out.at[to], dst_ref=into.at[col], send_sem=send_sem.at[to], recv_sem=recv_sem.at[col],
            device_id={"row": row, "col": to}, device_id_type=MESH).start()


def start_shared(both, send_sem, recv_sem, row, col):
    @pl.loop(1, 16)
    def _(d):
        to = (col + d) % 16
        pltpu.make_async_remote_copy(
            src_ref=both.at[col], dst_ref=both.at[col], send_sem=send_sem.at[to], recv_sem=recv_sem.at[col],
            device_id={"row": row, "col": to}, device_id_type=MESH).start()


def wait_on(ref, sem):
    pltpu.make_async_copy(ref, ref, sem).wait()


def finish_exchange(out, into, send_sem, recv_sem, col):
    @pl.loop(1, 16)
    def _(d):
        source = (col + d) % 16
        wait_on(into.at[source], recv_sem.at[source])
        wait_on(out.at[source], send_sem.at[source])

    into[col] = out[col]
    total = into[0].astype(jnp.float32)
    for c in range(1, 16):
        total = total + into[c].astype(jnp.float32)
    return total


def finish_shared(both, send_sem, recv_sem, col):
    @pl.loop(1, 16)
    def _(d):
        source = (col + d) % 16
        wait_on(both.at[source], recv_sem.at[source])
        wait_on(both.at[col], send_sem.at[source])

    return jnp.sum(both[...], axis=0)


def project_kernel(
    theta_ref, gate_ref, v_ref, sector_ref, offset_ref, kept_ref, fin_ref, out_ref, mask_ref,
    corr_out, corr_in, corr_diag_in, factor, gram_out, gram_in, gram_diag_in, th, bd, ap, vall, part, half_in, ring_in, quart, quart_in, done,
    th_sem, v_sem, v_send, v_recv, half_send, half_recv, ring_send, ring_recv,
    quart_send, quart_recv, fin_send, fin_recv, corr_send, corr_recv, corr_diag_send, corr_diag_recv,
    gram_send, gram_recv, gram_diag_send, gram_diag_recv, out_send, out_recv,
):
    row, col = lax.axis_index("row"), lax.axis_index("col")
    x, core = row // 2, row % 2
    y, z = col // 4, col % 4
    other = 1 - core

    def rows_at(step, which):
        return ((x + step) % 4) * 2 + which

    places = (
        row, rows_at(0, other), rows_at(3, core), rows_at(1, core),
        rows_at(3, other), rows_at(1, other), rows_at(2, core), rows_at(2, other),
    )
    sibling, before, after = places[1], places[2], places[3]

    def along(axis, step):
        if axis == 0:
            return {"row": row, "col": y * 4 + (z + step) % 4}
        return {"row": row, "col": ((y + step) % 4) * 4 + z}

    sends = []

    def send(src, dst, send_sem, recv_sem, where):
        copy = pltpu.make_async_remote_copy(
            src_ref=src, dst_ref=dst, send_sem=send_sem, recv_sem=recv_sem,
            device_id=where, device_id_type=MESH,
        )
        copy.start()
        sends.append(copy)

    def arrived(dst, sem):
        pltpu.make_async_copy(dst, dst, sem).wait()

    barrier = pltpu.get_barrier_semaphore()

    def greet(where):
        pl.semaphore_signal(barrier, inc=1, device_id=where, device_id_type=MESH)

    for where in (sibling, before, after):
        greet({"row": where, "col": col})

    @pl.loop(1, 16)
    def _(d):
        greet({"row": row, "col": (col + d) % 16})

    @pl.loop(1, 16)
    def _(d):
        greet({"row": col // 2, "col": (col + d) % 16})

    home = col // 2 == row

    @pl.when(jnp.logical_not(home))
    def _():
        greet({"row": col // 2, "col": col})

    theta_in = pltpu.make_async_copy(theta_ref, th.at[pl.ds(0, ROWS)], th_sem)
    theta_in.start()
    v_in = pltpu.make_async_copy(v_ref, vall.at[0], v_sem)
    v_in.start()

    big_r = lax.broadcasted_iota(jnp.int32, (256, 256), 0)
    big_c = lax.broadcasted_iota(jnp.int32, (256, 256), 1)
    left_hot = (lax.broadcasted_iota(jnp.int32, (256, 16), 0) // 16 == lax.broadcasted_iota(jnp.int32, (256, 16), 1))
    right_hot = (lax.broadcasted_iota(jnp.int32, (16, 256), 1) % 16 == lax.broadcasted_iota(jnp.int32, (16, 256), 0))
    spread = jnp.dot(left_hot.astype(jnp.bfloat16), gate_ref[...], preferred_element_type=jnp.float32)
    spread = jnp.dot(spread.astype(jnp.bfloat16), right_hot.astype(jnp.bfloat16), preferred_element_type=jnp.float32)
    bd[...] = jnp.where(big_r % 16 == big_c // 16, spread, 0.0).astype(jnp.bfloat16)
    th[pl.ds(ROWS, NMAX)] = jnp.zeros((NMAX, 16, LANES), jnp.bfloat16)
    pl.semaphore_wait(barrier, jnp.where(home, 33, 34))

    for s in range(2):
        for n, (where, place) in enumerate(((after, 2), (before, 3), (sibling, 1))):
            send(v_ref.at[s], vall.at[place, s], v_send.at[3 * s + n], v_recv.at[place, s], {"row": where, "col": col})
    theta_in.wait()
    v_in.wait()

    state = lax.broadcasted_iota(jnp.int32, (256, 256), 0) % 16
    state = state + 16 * (lax.broadcasted_iota(jnp.int32, (256, 256), 1) // LANES)

    def compute(u):
        place, s = ORDER[u]
        slot = places[place] * 2 + s
        if place:
            arrived(vall.at[place, s], v_recv.at[place, s])
            if place in (2, 3, 6):
                share = {2: 4, 3: 5, 6: 7}[place]
                if place == 2 and s == 0:
                    send(vall.at[2, 0], vall.at[6, 0], v_send.at[6], v_recv.at[6, 0], {"row": after, "col": col})
                if place == 3 and s == 1:
                    send(vall.at[3, 1], vall.at[6, 1], v_send.at[7], v_recv.at[6, 1], {"row": before, "col": col})
                n = 8 + 2 * (2, 3, 6).index(place) + s
                send(vall.at[place, s], vall.at[share, s], v_send.at[n], v_recv.at[share, s], {"row": sibling, "col": col})
        sector = sector_ref[slot]
        start = offset_ref[row, sector]
        end = jnp.where(sector == 15, ROWS, offset_ref[row, jnp.minimum(sector + 1, 15)])
        count = end - start
        for k in range(0, NMAX // 16, 2):
            both = th[pl.ds(start + 16 * k, 32)].reshape(512, LANES)
            both = jnp.concatenate([both[:256], both[256:]], axis=1)
            gated = jnp.dot(bd[...], both, preferred_element_type=jnp.float32)
            gated = jnp.where(state + 16 * k < count, gated, 0.0).astype(jnp.bfloat16)
            for a in range(SITES):
                for b in range(SITES):
                    for m in range(2):
                        ap[a * NMAX + 16 * (k + m): a * NMAX + 16 * (k + m + 1), b * LANES:(b + 1) * LANES] = gated[
                            (a * 4 + b) * 16:(a * 4 + b + 1) * 16, m * LANES:(m + 1) * LANES]
        product = jnp.dot(ap[...], vall[place, s], preferred_element_type=jnp.float32).astype(jnp.bfloat16)
        for a in range(SITES):
            part[u, a] = product[a * NMAX:(a + 1) * NMAX]
        axis = u % 2
        mine = z if axis == 0 else y
        far = (mine + 2) % 4
        send(part.at[u, far, pl.ds(0, HALF)], half_in.at[u, 0], half_send.at[u, 0], half_recv.at[u, 0], along(axis, 1))
        send(part.at[u, far, pl.ds(HALF, HALF)], half_in.at[u, 1], half_send.at[u, 1], half_recv.at[u, 1], along(axis, 3))

    def pass_on(u):
        axis = u % 2
        mine = z if axis == 0 else y
        for n, step in ((0, 1), (1, 3)):
            arrived(half_in.at[u, n], half_recv.at[u, n])
            to = (mine + step) % 4
            rows = pl.ds(n * HALF, HALF)
            total = part[u, to, rows, :].astype(jnp.float32) + half_in[u, n].astype(jnp.float32)
            part[u, to, rows, :] = total.astype(jnp.bfloat16)
            send(part.at[u, to], ring_in.at[u, n], ring_send.at[u, n], ring_recv.at[u, n], along(axis, step))

    def split(u):
        axis = u % 2
        mine = z if axis == 0 else y
        second = y if axis == 0 else z
        for n in range(2):
            arrived(ring_in.at[u, n], ring_recv.at[u, n])
        total = part[u, mine].astype(jnp.float32) + ring_in[u, 0].astype(jnp.float32) + ring_in[u, 1].astype(jnp.float32)
        total = total.astype(jnp.bfloat16)
        for q in range(4):
            quart[u, q] = total[:, q * LANES:(q + 1) * LANES]
        for d in (2, 1, 3):
            send(quart.at[u, (second + d) % 4], quart_in.at[u, d - 1], quart_send.at[u, d - 1],
                 quart_recv.at[u, d - 1], along(1 - axis, d))

    def finish(u):
        axis = u % 2
        place, s = ORDER[u]
        mine = z if axis == 0 else y
        second = y if axis == 0 else z
        total = quart[u, second].astype(jnp.float32)
        for d in (1, 2, 3):
            arrived(quart_in.at[u, d - 1], quart_recv.at[u, d - 1])
            total = total + quart_in[u, d - 1].astype(jnp.float32)
        done[u] = total.astype(jnp.bfloat16)
        for h in range(2):
            src = done.at[u, pl.ds(h * HALF, HALF)]
            dst = fin_ref.at[s, mine, second]
            target = 2 * row + h
            if place == 0:
                @pl.when(col == target)
                def _():
                    pltpu.make_async_copy(src, dst, fin_recv.at[s, col]).start()

                @pl.when(col != target)
                def _():
                    pltpu.make_async_remote_copy(
                        src_ref=src, dst_ref=dst, send_sem=fin_send.at[u, h], recv_sem=fin_recv.at[s, col],
                        device_id={"row": places[place], "col": target}, device_id_type=MESH).start()
            else:
                send(src, dst, fin_send.at[u, h], fin_recv.at[s, col], {"row": places[place], "col": target})

    def each(task, group):
        if 0 <= group < 4:
            for u in range(4 * group, 4 * group + 4):
                task(u)

    for group in range(7):
        each(compute, group)
        if group == 0:
            overlap(vall.at[0], corr_out, corr_diag_in, row, col)
            start_exchange(corr_out, corr_in, corr_send, corr_recv, row, col)
            start_shared(corr_diag_in, corr_diag_send, corr_diag_recv, row, col)
        each(finish, group - 2)
        each(split, group - 1)
        each(pass_on, group)
    correlation = finish_exchange(corr_out, corr_in, corr_send, corr_recv, col)
    corr_diag = finish_shared(corr_diag_in, corr_diag_send, corr_diag_recv, col)

    for s in range(2):
        @pl.loop(0, 16)
        def _(c):
            arrived(fin_ref.at[s, 0, 0], fin_recv.at[s, c])

    for s in range(2):
        for a in range(SITES):
            for q in range(4):
                factor[s, a * HALF:(a + 1) * HALF, q * LANES:(q + 1) * LANES] = fin_ref[s, a, q]
    overlap(factor, gram_out, gram_diag_in, row, col)
    start_shared(gram_diag_in, gram_diag_send, gram_diag_recv, row, col)
    start_exchange(gram_out, gram_in, gram_send, gram_recv, row, col)
    gram_diag = finish_shared(gram_diag_in, gram_diag_send, gram_diag_recv, col)
    lambdas = gram_diag / (corr_diag + 1e-06)
    gram = finish_exchange(gram_out, gram_in, gram_send, gram_recv, col)
    at_row = lax.broadcasted_iota(jnp.int32, (SHARE, KEPT), 0) + SHARE * col
    at_col = lax.broadcasted_iota(jnp.int32, (SHARE, KEPT), 1)
    for s in range(2):
        kept = kept_ref[sector_ref[2 * row + s]]
        across = jnp.concatenate([lambdas[s * 4 + q:s * 4 + q + 1] for q in range(4)], axis=1)
        norms = jnp.concatenate([corr_diag[s * 4 + q:s * 4 + q + 1] for q in range(4)], axis=1)
        across = jnp.broadcast_to(across, (SHARE, KEPT))
        down = jnp.sum(jnp.where(at_row == at_col, across, 0.0), axis=1, keepdims=True)
        differ = across - down
        mean = DAMPING * (across + down)
        divisor = differ * differ + mean * mean + 1e-06
        offdiag = (gram[s] - across * correlation[s]) * differ / divisor
        result = jnp.where(at_row == at_col, 0.5 * (1.0 - norms), offdiag)
        result = jnp.where((at_row < kept) & (at_col < kept), result, 0.0)
        out_ref[s, col] = result.astype(jnp.bfloat16)
        lanes = lax.broadcasted_iota(jnp.int32, (8, KEPT), 1)
        mask_ref[s] = jnp.where(lanes < kept, 1.0, 0.0)

    @pl.loop(1, 16)
    def _(d):
        to = (col + d) % 16
        pltpu.make_async_remote_copy(
            src_ref=out_ref.at[:, col], dst_ref=out_ref.at[:, col], send_sem=out_send.at[to],
            recv_sem=out_recv.at[col], device_id={"row": row, "col": to}, device_id_type=MESH).start()

    @pl.loop(1, 16)
    def _(d):
        source = (col + d) % 16
        wait_on(out_ref.at[:, source], out_recv.at[source])
        wait_on(out_ref.at[:, col], out_send.at[source])

    for copy in sends:
        copy.wait_send()
    for s in range(2):
        for h in range(2):
            @pl.when(col != 2 * row + h)
            def _():
                pltpu.make_async_copy(done.at[s, pl.ds(h * HALF, HALF)], done.at[s, pl.ds(h * HALF, HALF)], fin_send.at[s, h]).wait()


def project(theta, gate, vectors, slot_sector, block_offsets, kept):
    bf = jnp.bfloat16
    dma = pltpu.SemaphoreType.DMA
    vmem = pl.BlockSpec(memory_space=pltpu.VMEM)
    smem = pl.BlockSpec(memory_space=pltpu.SMEM)
    hbm = pl.BlockSpec(memory_space=pl.ANY)
    return pl.pallas_call(
        project_kernel,
        out_shape=(
            jax.ShapeDtypeStruct((2, SITES, 4, HALF, LANES), bf),
            jax.ShapeDtypeStruct((2, 16, SHARE, KEPT), bf),
            jax.ShapeDtypeStruct((2, 8, KEPT), jnp.float32),
        ),
        in_specs=[hbm, vmem, hbm, smem, smem, smem],
        out_specs=(vmem, vmem, vmem),
        scratch_shapes=[
            pltpu.VMEM((16, 2, SHARE, KEPT), bf),
            pltpu.VMEM((16, 2, SHARE, KEPT), bf),
            pltpu.VMEM((16, 8, LANES), jnp.float32),
            pltpu.VMEM((2, SITES * HALF, KEPT), bf),
            pltpu.VMEM((16, 2, SHARE, KEPT), bf),
            pltpu.VMEM((16, 2, SHARE, KEPT), bf),
            pltpu.VMEM((16, 8, LANES), jnp.float32),
            pltpu.VMEM((ROWS + NMAX, 16, LANES), bf),
            pltpu.VMEM((256, 256), bf),
            pltpu.VMEM((SITES * NMAX, KEPT), bf),
            pltpu.VMEM((8, 2, KEPT, KEPT), bf),
            pltpu.VMEM((UNITS, SITES, NMAX, KEPT), bf),
            pltpu.VMEM((UNITS, 2, HALF, KEPT), bf),
            pltpu.VMEM((UNITS, 2, NMAX, KEPT), bf),
            pltpu.VMEM((UNITS, 4, NMAX, LANES), bf),
            pltpu.VMEM((UNITS, 3, NMAX, LANES), bf),
            pltpu.VMEM((UNITS, NMAX, LANES), bf),
            dma, dma, dma((14,)), dma((8, 2)),
            dma((UNITS, 2)), dma((UNITS, 2)), dma((UNITS, 2)), dma((UNITS, 2)),
            dma((UNITS, 3)), dma((UNITS, 3)), dma((UNITS, 2)), dma((2, 16)),
        ] + [dma((16,))] * 10,
        compiler_params=pltpu.CompilerParams(has_side_effects=True, collective_id=0, vmem_limit_bytes=56 * 2**20),
        cost_estimate=pl.CostEstimate(flops=5_000_000_000, bytes_accessed=6_000_000, transcendentals=0),
        name="project",
    )(theta, gate, vectors, slot_sector, block_offsets, kept)


def shards(theta, gate, warm_start, slot_sector, kept, block_offsets):
    vectors = warm_start.reshape(2, KEPT, KEPT)
    fin, corr_b, mask = project(
        theta.reshape(ROWS, 16, LANES), gate.reshape(16, 16), vectors, slot_sector, block_offsets, kept
    )
    corr_b = corr_b.reshape(2, KEPT, KEPT)
    kept_mask = mask[:, 0]
    projected_b = fin.transpose(0, 1, 3, 2, 4).reshape(2, SITES * HALF, KEPT)
    new_vectors = vectors.astype(jnp.float32) + jnp.einsum(
        "snk,skl->snl", vectors, corr_b, preferred_element_type=jnp.float32
    )
    new_vectors = new_vectors * kept_mask[:, None, :]
    left = projected_b.astype(jnp.float32) + jnp.einsum(
        "snk,skl->snl", projected_b, corr_b, preferred_element_type=jnp.float32
    )
    left = left * kept_mask[:, None, :]
    left = left.reshape(2, SITES, HALF, KEPT).transpose(2, 0, 1, 3)
    return (left, new_vectors.reshape(2, 4, LANES, KEPT))


def solution(mesh):
    in_specs = (P("row", None, None, "col"), P(), P("row", None, "col", None), P(), P(), P())
    out_specs = (P("col", "row", None, None), P("row", None, "col", None))
    return jax.shard_map(shards, mesh=mesh, in_specs=in_specs, out_specs=out_specs, check_vma=False)
```

```python
import jax
import jax.numpy as jnp
from jax import lax
from jax.experimental import pallas as pl
from jax.experimental.pallas import tpu as pltpu
from jax.sharding import PartitionSpec as P

NMAX = 96
HALF = NMAX // 2
SITES = 4
LANES = 128
SHARE = 32
KEPT = 512
ROWS = 1024
DAMPING = 0.25
MESH = pl.DeviceIdType.MESH

ORDER = (
    (0, 0), (1, 0), (0, 1), (1, 1),
    (2, 0), (3, 0), (4, 0), (5, 0),
    (6, 0), (7, 0), (3, 1), (5, 1),
    (2, 1), (6, 1), (4, 1), (7, 1),
)
UNITS = len(ORDER)


def overlap(block, out, diag, col):
    product = lax.dot_general(block, block, (((0,), (0,)), ((), ())), preferred_element_type=jnp.float32)
    product = product.astype(jnp.bfloat16)
    for c in range(16):
        out[c] = product[c * SHARE:(c + 1) * SHARE]
    wide = block.astype(jnp.float32)
    squares = jnp.sum(wide * wide, axis=0, keepdims=True)
    for q in range(4):
        diag[col, q:q + 1] = squares[:, q * LANES:(q + 1) * LANES]


def start_exchange(out, into, send_sem, recv_sem, row, col):
    @pl.loop(1, 16)
    def _(d):
        to = (col + d) % 16
        pltpu.make_async_remote_copy(
            src_ref=out.at[to], dst_ref=into.at[col], send_sem=send_sem.at[to], recv_sem=recv_sem.at[col],
            device_id={"row": row, "col": to}, device_id_type=MESH).start()


def start_shared(both, send_sem, recv_sem, row, col):
    @pl.loop(1, 16)
    def _(d):
        to = (col + d) % 16
        pltpu.make_async_remote_copy(
            src_ref=both.at[col], dst_ref=both.at[col], send_sem=send_sem.at[to], recv_sem=recv_sem.at[col],
            device_id={"row": row, "col": to}, device_id_type=MESH).start()


def wait_on(ref, sem):
    pltpu.make_async_copy(ref, ref, sem).wait()


def finish_exchange(out, into, send_sem, recv_sem, col):
    @pl.loop(1, 16)
    def _(d):
        source = (col + d) % 16
        wait_on(into.at[source], recv_sem.at[source])
        wait_on(out.at[source], send_sem.at[source])

    into[col] = out[col]
    total = into[0].astype(jnp.float32)
    for c in range(1, 16):
        total = total + into[c].astype(jnp.float32)
    return total


def finish_shared(both, send_sem, recv_sem, col):
    @pl.loop(1, 16)
    def _(d):
        source = (col + d) % 16
        wait_on(both.at[source], recv_sem.at[source])
        wait_on(both.at[col], send_sem.at[source])

    return jnp.sum(both[...], axis=0)


def project_kernel(
    theta_ref, gate_ref, v_ref, sector_ref, offset_ref, kept_ref, fin_ref, out_ref, mask_ref,
    corr_out, corr_in, corr_diag_in, factor, gram_out, gram_in, gram_diag_in, th, bd, ap, vall, part, half_in, ring_in, quart, quart_in, done,
    th_sem, v_sem, v_send, v_recv, half_send, half_recv, ring_send, ring_recv,
    quart_send, quart_recv, fin_send, fin_recv, corr_send, corr_recv, corr_diag_send, corr_diag_recv,
    gram_send, gram_recv, gram_diag_send, gram_diag_recv, out_send, out_recv,
):
    row, col = lax.axis_index("row"), lax.axis_index("col")
    x, core = row // 2, row % 2
    y, z = col // 4, col % 4
    other = 1 - core

    def rows_at(step, which):
        return ((x + step) % 4) * 2 + which

    places = (
        row, rows_at(0, other), rows_at(3, core), rows_at(1, core),
        rows_at(3, other), rows_at(1, other), rows_at(2, core), rows_at(2, other),
    )
    sibling, before, after = places[1], places[2], places[3]

    def along(axis, step):
        if axis == 0:
            return {"row": row, "col": y * 4 + (z + step) % 4}
        return {"row": row, "col": ((y + step) % 4) * 4 + z}

    sends = []

    def send(src, dst, send_sem, recv_sem, where):
        copy = pltpu.make_async_remote_copy(
            src_ref=src, dst_ref=dst, send_sem=send_sem, recv_sem=recv_sem,
            device_id=where, device_id_type=MESH,
        )
        copy.start()
        sends.append(copy)

    def arrived(dst, sem):
        pltpu.make_async_copy(dst, dst, sem).wait()

    barrier = pltpu.get_barrier_semaphore()

    def greet(where):
        pl.semaphore_signal(barrier, inc=1, device_id=where, device_id_type=MESH)

    for where in (sibling, before, after):
        greet({"row": where, "col": col})

    @pl.loop(1, 16)
    def _(d):
        greet({"row": row, "col": (col + d) % 16})

    @pl.loop(1, 16)
    def _(d):
        greet({"row": col // 2, "col": (col + d) % 16})

    home = col // 2 == row

    @pl.when(jnp.logical_not(home))
    def _():
        greet({"row": col // 2, "col": col})

    theta_in = pltpu.make_async_copy(theta_ref, th.at[pl.ds(0, ROWS)], th_sem)
    theta_in.start()
    v_in = pltpu.make_async_copy(v_ref, vall.at[0], v_sem)
    v_in.start()

    big_r = lax.broadcasted_iota(jnp.int32, (256, 256), 0)
    big_c = lax.broadcasted_iota(jnp.int32, (256, 256), 1)
    left_hot = (lax.broadcasted_iota(jnp.int32, (256, 16), 0) // 16 == lax.broadcasted_iota(jnp.int32, (256, 16), 1))
    right_hot = (lax.broadcasted_iota(jnp.int32, (16, 256), 1) % 16 == lax.broadcasted_iota(jnp.int32, (16, 256), 0))
    spread = jnp.dot(left_hot.astype(jnp.bfloat16), gate_ref[...], preferred_element_type=jnp.float32)
    spread = jnp.dot(spread.astype(jnp.bfloat16), right_hot.astype(jnp.bfloat16), preferred_element_type=jnp.float32)
    bd[...] = jnp.where(big_r % 16 == big_c // 16, spread, 0.0).astype(jnp.bfloat16)
    th[pl.ds(ROWS, NMAX)] = jnp.zeros((NMAX, 16, LANES), jnp.bfloat16)
    pl.semaphore_wait(barrier, jnp.where(home, 33, 34))

    def send_own(s, n):
        where, place = ((after, 2), (before, 3), (sibling, 1))[n]
        send(v_ref.at[s], vall.at[place, s], v_send.at[3 * s + n], v_recv.at[place, s], {"row": where, "col": col})

    for s, n in ((0, 2), (0, 0), (0, 1), (1, 2)):
        send_own(s, n)
    theta_in.wait()
    v_in.wait()

    state = lax.broadcasted_iota(jnp.int32, (256, 256), 0) % 16
    state = state + 16 * (lax.broadcasted_iota(jnp.int32, (256, 256), 1) // LANES)

    def compute(u):
        place, s = ORDER[u]
        slot = places[place] * 2 + s
        if place:
            arrived(vall.at[place, s], v_recv.at[place, s])
            if place in (2, 3, 6):
                share = {2: 4, 3: 5, 6: 7}[place]
                if place == 2 and s == 0:
                    send(vall.at[2, 0], vall.at[6, 0], v_send.at[6], v_recv.at[6, 0], {"row": after, "col": col})
                if place == 3 and s == 1:
                    send(vall.at[3, 1], vall.at[6, 1], v_send.at[7], v_recv.at[6, 1], {"row": before, "col": col})
                n = 8 + 2 * (2, 3, 6).index(place) + s
                send(vall.at[place, s], vall.at[share, s], v_send.at[n], v_recv.at[share, s], {"row": sibling, "col": col})
        sector = sector_ref[slot]
        start = offset_ref[row, sector]
        end = jnp.where(sector == 15, ROWS, offset_ref[row, jnp.minimum(sector + 1, 15)])
        count = end - start
        for k in range(0, NMAX // 16, 2):
            both = th[pl.ds(start + 16 * k, 32)].reshape(512, LANES)
            both = jnp.concatenate([both[:256], both[256:]], axis=1)
            gated = jnp.dot(bd[...], both, preferred_element_type=jnp.float32)
            gated = jnp.where(state + 16 * k < count, gated, 0.0).astype(jnp.bfloat16)
            for a in range(SITES):
                for b in range(SITES):
                    for m in range(2):
                        ap[a * NMAX + 16 * (k + m): a * NMAX + 16 * (k + m + 1), b * LANES:(b + 1) * LANES] = gated[
                            (a * 4 + b) * 16:(a * 4 + b + 1) * 16, m * LANES:(m + 1) * LANES]
        product = jnp.dot(ap[...], vall[place, s], preferred_element_type=jnp.float32).astype(jnp.bfloat16)
        for a in range(SITES):
            part[u, a] = product[a * NMAX:(a + 1) * NMAX]
        axis = u % 2
        mine = z if axis == 0 else y
        far = (mine + 2) % 4
        send(part.at[u, far, pl.ds(0, HALF)], half_in.at[u, 0], half_send.at[u, 0], half_recv.at[u, 0], along(axis, 1))
        send(part.at[u, far, pl.ds(HALF, HALF)], half_in.at[u, 1], half_send.at[u, 1], half_recv.at[u, 1], along(axis, 3))

    def pass_on(u):
        axis = u % 2
        mine = z if axis == 0 else y
        for n, step in ((0, 1), (1, 3)):
            arrived(half_in.at[u, n], half_recv.at[u, n])
            to = (mine + step) % 4
            rows = pl.ds(n * HALF, HALF)
            total = part[u, to, rows, :].astype(jnp.float32) + half_in[u, n].astype(jnp.float32)
            part[u, to, rows, :] = total.astype(jnp.bfloat16)
            send(part.at[u, to], ring_in.at[u, n], ring_send.at[u, n], ring_recv.at[u, n], along(axis, step))

    def split(u):
        axis = u % 2
        mine = z if axis == 0 else y
        second = y if axis == 0 else z
        for n in range(2):
            arrived(ring_in.at[u, n], ring_recv.at[u, n])
        total = part[u, mine].astype(jnp.float32) + ring_in[u, 0].astype(jnp.float32) + ring_in[u, 1].astype(jnp.float32)
        total = total.astype(jnp.bfloat16)
        for q in range(4):
            quart[u, q] = total[:, q * LANES:(q + 1) * LANES]
        for d in (2, 1, 3):
            send(quart.at[u, (second + d) % 4], quart_in.at[u, d - 1], quart_send.at[u, d - 1],
                 quart_recv.at[u, d - 1], along(1 - axis, d))

    def finish(u):
        axis = u % 2
        place, s = ORDER[u]
        mine = z if axis == 0 else y
        second = y if axis == 0 else z
        total = quart[u, second].astype(jnp.float32)
        for d in (1, 2, 3):
            arrived(quart_in.at[u, d - 1], quart_recv.at[u, d - 1])
            total = total + quart_in[u, d - 1].astype(jnp.float32)
        done[u] = total.astype(jnp.bfloat16)
        for h in range(2):
            src = done.at[u, pl.ds(h * HALF, HALF)]
            dst = fin_ref.at[s, mine, second]
            target = 2 * row + h
            if place == 0:
                @pl.when(col == target)
                def _():
                    pltpu.make_async_copy(src, dst, fin_recv.at[s, col]).start()

                @pl.when(col != target)
                def _():
                    pltpu.make_async_remote_copy(
                        src_ref=src, dst_ref=dst, send_sem=fin_send.at[u, h], recv_sem=fin_recv.at[s, col],
                        device_id={"row": places[place], "col": target}, device_id_type=MESH).start()
            else:
                send(src, dst, fin_send.at[u, h], fin_recv.at[s, col], {"row": places[place], "col": target})

    def each(task, group):
        if 0 <= group < 4:
            for u in range(4 * group, 4 * group + 4):
                task(u)

    at_row = lax.broadcasted_iota(jnp.int32, (SHARE, KEPT), 0) + SHARE * col
    at_col = lax.broadcasted_iota(jnp.int32, (SHARE, KEPT), 1)

    def start_corr():
        for s in range(2):
            overlap(vall[0, s], corr_out.at[s], corr_diag_in.at[s], col)
            start_shared(corr_diag_in.at[s], corr_diag_send.at[s], corr_diag_recv.at[s], row, col)
            start_exchange(corr_out.at[s], corr_in.at[s], corr_send.at[s], corr_recv.at[s], row, col)

    def start_gram(s):
        @pl.loop(0, 16)
        def _(c):
            arrived(fin_ref.at[s, 0, 0], fin_recv.at[s, c])

        for a in range(SITES):
            for q in range(4):
                factor[s, a * HALF:(a + 1) * HALF, q * LANES:(q + 1) * LANES] = fin_ref[s, a, q]
        overlap(factor[s], gram_out.at[s], gram_diag_in.at[s], col)
        start_shared(gram_diag_in.at[s], gram_diag_send.at[s], gram_diag_recv.at[s], row, col)
        start_exchange(gram_out.at[s], gram_in.at[s], gram_send.at[s], gram_recv.at[s], row, col)

    def refine(s):
        correlation = finish_exchange(corr_out.at[s], corr_in.at[s], corr_send.at[s], corr_recv.at[s], col)
        corr_diag = finish_shared(corr_diag_in.at[s], corr_diag_send.at[s], corr_diag_recv.at[s], col)
        gram_diag = finish_shared(gram_diag_in.at[s], gram_diag_send.at[s], gram_diag_recv.at[s], col)
        lambdas = gram_diag / (corr_diag + 1e-06)
        gram = finish_exchange(gram_out.at[s], gram_in.at[s], gram_send.at[s], gram_recv.at[s], col)
        kept = kept_ref[sector_ref[2 * row + s]]
        across = jnp.concatenate([lambdas[q:q + 1] for q in range(4)], axis=1)
        norms = jnp.concatenate([corr_diag[q:q + 1] for q in range(4)], axis=1)
        across = jnp.broadcast_to(across, (SHARE, KEPT))
        down = jnp.sum(jnp.where(at_row == at_col, across, 0.0), axis=1, keepdims=True)
        differ = across - down
        mean = DAMPING * (across + down)
        divisor = differ * differ + mean * mean + 1e-06
        offdiag = (gram - across * correlation) * differ / divisor
        result = jnp.where(at_row == at_col, 0.5 * (1.0 - norms), offdiag)
        result = jnp.where((at_row < kept) & (at_col < kept), result, 0.0)
        out_ref[s, col] = result.astype(jnp.bfloat16)
        lanes = lax.broadcasted_iota(jnp.int32, (8, KEPT), 1)
        mask_ref[s] = jnp.where(lanes < kept, 1.0, 0.0)
        start_shared(out_ref.at[s], out_send.at[s], out_recv.at[s], row, col)

    each(compute, 0)
    start_corr()
    each(pass_on, 0)
    send_own(1, 1)
    each(compute, 1)
    each(split, 0)
    send_own(1, 0)
    each(pass_on, 1)
    each(finish, 0)
    each(compute, 2)
    each(split, 1)
    each(pass_on, 2)
    each(finish, 1)
    each(split, 2)
    each(compute, 3)
    each(finish, 2)
    each(pass_on, 3)
    start_gram(0)
    each(split, 3)
    each(finish, 3)
    refine(0)
    start_gram(1)
    refine(1)
    for s in range(2):
        @pl.loop(1, 16)
        def _(d):
            source = (col + d) % 16
            wait_on(out_ref.at[s, source], out_recv.at[s, source])
            wait_on(out_ref.at[s, col], out_send.at[s, source])

    for copy in sends:
        copy.wait_send()
    for s in range(2):
        for h in range(2):
            @pl.when(col != 2 * row + h)
            def _():
                pltpu.make_async_copy(done.at[s, pl.ds(h * HALF, HALF)], done.at[s, pl.ds(h * HALF, HALF)], fin_send.at[2 * s, h]).wait()


def project(theta, gate, vectors, slot_sector, block_offsets, kept):
    bf = jnp.bfloat16
    dma = pltpu.SemaphoreType.DMA
    vmem = pl.BlockSpec(memory_space=pltpu.VMEM)
    smem = pl.BlockSpec(memory_space=pltpu.SMEM)
    hbm = pl.BlockSpec(memory_space=pl.ANY)
    return pl.pallas_call(
        project_kernel,
        out_shape=(
            jax.ShapeDtypeStruct((2, SITES, 4, HALF, LANES), bf),
            jax.ShapeDtypeStruct((2, 16, SHARE, KEPT), bf),
            jax.ShapeDtypeStruct((2, 8, KEPT), jnp.float32),
        ),
        in_specs=[hbm, vmem, hbm, smem, smem, smem],
        out_specs=(vmem, vmem, vmem),
        scratch_shapes=[
            pltpu.VMEM((2, 16, SHARE, KEPT), bf),
            pltpu.VMEM((2, 16, SHARE, KEPT), bf),
            pltpu.VMEM((2, 16, 8, LANES), jnp.float32),
            pltpu.VMEM((2, SITES * HALF, KEPT), bf),
            pltpu.VMEM((2, 16, SHARE, KEPT), bf),
            pltpu.VMEM((2, 16, SHARE, KEPT), bf),
            pltpu.VMEM((2, 16, 8, LANES), jnp.float32),
            pltpu.VMEM((ROWS + NMAX, 16, LANES), bf),
            pltpu.VMEM((256, 256), bf),
            pltpu.VMEM((SITES * NMAX, KEPT), bf),
            pltpu.VMEM((8, 2, KEPT, KEPT), bf),
            pltpu.VMEM((UNITS, SITES, NMAX, KEPT), bf),
            pltpu.VMEM((UNITS, 2, HALF, KEPT), bf),
            pltpu.VMEM((UNITS, 2, NMAX, KEPT), bf),
            pltpu.VMEM((UNITS, 4, NMAX, LANES), bf),
            pltpu.VMEM((UNITS, 3, NMAX, LANES), bf),
            pltpu.VMEM((UNITS, NMAX, LANES), bf),
            dma, dma, dma((14,)), dma((8, 2)),
            dma((UNITS, 2)), dma((UNITS, 2)), dma((UNITS, 2)), dma((UNITS, 2)),
            dma((UNITS, 3)), dma((UNITS, 3)), dma((UNITS, 2)), dma((2, 16)),
        ] + [dma((2, 16))] * 10,
        compiler_params=pltpu.CompilerParams(has_side_effects=True, collective_id=0, vmem_limit_bytes=56 * 2**20),
        cost_estimate=pl.CostEstimate(flops=5_000_000_000, bytes_accessed=6_000_000, transcendentals=0),
        name="project",
    )(theta, gate, vectors, slot_sector, block_offsets, kept)


def shards(theta, gate, warm_start, slot_sector, kept, block_offsets):
    vectors = warm_start.reshape(2, KEPT, KEPT)
    fin, corr_b, mask = project(
        theta.reshape(ROWS, 16, LANES), gate.reshape(16, 16), vectors, slot_sector, block_offsets, kept
    )
    corr_b = corr_b.reshape(2, KEPT, KEPT)
    kept_mask = mask[:, 0]
    projected_b = fin.transpose(0, 1, 3, 2, 4).reshape(2, SITES * HALF, KEPT)
    new_vectors = vectors.astype(jnp.float32) + jnp.einsum(
        "snk,skl->snl", vectors, corr_b, preferred_element_type=jnp.float32
    )
    new_vectors = new_vectors * kept_mask[:, None, :]
    left = projected_b.astype(jnp.float32) + jnp.einsum(
        "snk,skl->snl", projected_b, corr_b, preferred_element_type=jnp.float32
    )
    left = left * kept_mask[:, None, :]
    left = left.reshape(2, SITES, HALF, KEPT).transpose(2, 0, 1, 3)
    return (left, new_vectors.reshape(2, 4, LANES, KEPT))


def solution(mesh):
    in_specs = (P("row", None, None, "col"), P(), P("row", None, "col", None), P(), P(), P())
    out_specs = (P("col", "row", None, None), P("row", None, "col", None))
    return jax.shard_map(shards, mesh=mesh, in_specs=in_specs, out_specs=out_specs, check_vma=False)
```

```python
import jax
import jax.numpy as jnp
from jax import lax
from jax.experimental import pallas as pl
from jax.experimental.pallas import tpu as pltpu
from jax.sharding import PartitionSpec as P

NMAX = 96
HALF = NMAX // 2
SITES = 4
LANES = 128
SHARE = 32
KEPT = 512
ROWS = 1024
DAMPING = 0.25
MESH = pl.DeviceIdType.MESH

ORDER = (
    (0, 0), (1, 0), (0, 1), (1, 1),
    (2, 0), (3, 0), (4, 0), (5, 0),
    (6, 0), (7, 0), (3, 1), (5, 1),
    (2, 1), (6, 1), (4, 1), (7, 1),
)
UNITS = len(ORDER)


def overlap(block, out, diag, col):
    product = lax.dot_general(block, block, (((0,), (0,)), ((), ())), preferred_element_type=jnp.float32)
    product = product.astype(jnp.bfloat16)
    for c in range(16):
        out[c] = product[c * SHARE:(c + 1) * SHARE]
    wide = block.astype(jnp.float32)
    squares = jnp.sum(wide * wide, axis=0, keepdims=True)
    for q in range(4):
        diag[col, q:q + 1] = squares[:, q * LANES:(q + 1) * LANES]


def start_exchange(out, into, send_sem, recv_sem, row, col):
    @pl.loop(1, 16)
    def _(d):
        to = (col + d) % 16
        pltpu.make_async_remote_copy(
            src_ref=out.at[to], dst_ref=into.at[col], send_sem=send_sem.at[to], recv_sem=recv_sem.at[col],
            device_id={"row": row, "col": to}, device_id_type=MESH).start()


def start_shared(both, send_sem, recv_sem, row, col):
    @pl.loop(1, 16)
    def _(d):
        to = (col + d) % 16
        pltpu.make_async_remote_copy(
            src_ref=both.at[col], dst_ref=both.at[col], send_sem=send_sem.at[to], recv_sem=recv_sem.at[col],
            device_id={"row": row, "col": to}, device_id_type=MESH).start()


def wait_on(ref, sem):
    pltpu.make_async_copy(ref, ref, sem).wait()


def finish_exchange(out, into, send_sem, recv_sem, col):
    @pl.loop(1, 16)
    def _(d):
        source = (col + d) % 16
        wait_on(into.at[source], recv_sem.at[source])
        wait_on(out.at[source], send_sem.at[source])

    into[col] = out[col]
    total = into[0].astype(jnp.float32)
    for c in range(1, 16):
        total = total + into[c].astype(jnp.float32)
    return total


def finish_shared(both, send_sem, recv_sem, col):
    @pl.loop(1, 16)
    def _(d):
        source = (col + d) % 16
        wait_on(both.at[source], recv_sem.at[source])
        wait_on(both.at[col], send_sem.at[source])

    return jnp.sum(both[...], axis=0)


def project_kernel(
    theta_ref, gate_ref, v_ref, sector_ref, offset_ref, kept_ref, fin_ref, out_ref,
    corr_out, corr_in, corr_diag_in, factor, gram_out, gram_in, gram_diag_in, th, bd, ap, vall, part, half_in, ring_in, quart, quart_in, done,
    th_sem, v_sem, v_send, v_recv, half_send, half_recv, ring_send, ring_recv,
    quart_send, quart_recv, fin_send, fin_recv, corr_send, corr_recv, corr_diag_send, corr_diag_recv,
    gram_send, gram_recv, gram_diag_send, gram_diag_recv, out_send, out_recv,
):
    row, col = lax.axis_index("row"), lax.axis_index("col")
    x, core = row // 2, row % 2
    y, z = col // 4, col % 4
    other = 1 - core

    def rows_at(step, which):
        return ((x + step) % 4) * 2 + which

    places = (
        row, rows_at(0, other), rows_at(3, core), rows_at(1, core),
        rows_at(3, other), rows_at(1, other), rows_at(2, core), rows_at(2, other),
    )
    sibling, before, after = places[1], places[2], places[3]

    def along(axis, step):
        if axis == 0:
            return {"row": row, "col": y * 4 + (z + step) % 4}
        return {"row": row, "col": ((y + step) % 4) * 4 + z}

    sends = []

    def send(src, dst, send_sem, recv_sem, where):
        copy = pltpu.make_async_remote_copy(
            src_ref=src, dst_ref=dst, send_sem=send_sem, recv_sem=recv_sem,
            device_id=where, device_id_type=MESH,
        )
        copy.start()
        sends.append(copy)

    def arrived(dst, sem):
        pltpu.make_async_copy(dst, dst, sem).wait()

    barrier = pltpu.get_barrier_semaphore()

    def greet(where):
        pl.semaphore_signal(barrier, inc=1, device_id=where, device_id_type=MESH)

    for where in (sibling, before, after):
        greet({"row": where, "col": col})

    @pl.loop(1, 16)
    def _(d):
        greet({"row": row, "col": (col + d) % 16})

    @pl.loop(1, 16)
    def _(d):
        greet({"row": col // 2, "col": (col + d) % 16})

    home = col // 2 == row

    @pl.when(jnp.logical_not(home))
    def _():
        greet({"row": col // 2, "col": col})

    theta_in = pltpu.make_async_copy(theta_ref, th.at[pl.ds(0, ROWS)], th_sem)
    theta_in.start()
    v_in = pltpu.make_async_copy(v_ref, vall.at[0], v_sem)
    v_in.start()

    pair_r = lax.broadcasted_iota(jnp.int32, (4, 256), 0)
    pair_c = lax.broadcasted_iota(jnp.int32, (4, 256), 1)
    second_in = (pair_r == pair_c % 4).astype(jnp.bfloat16)
    same = lax.broadcasted_iota(jnp.int32, (16, 256), 0) == lax.broadcasted_iota(jnp.int32, (16, 256), 1) // 16
    for a in range(4):
        for b in range(4):
            spread = jnp.dot(gate_ref[a, b], second_in, preferred_element_type=jnp.float32)
            spread = jnp.sum(jnp.where(pair_r == pair_c // 4 % 4, spread, 0.0), axis=0, keepdims=True)
            spread = jnp.where(same, jnp.broadcast_to(spread, (16, 256)), 0.0)
            bd[(a * 4 + b) * 16:(a * 4 + b + 1) * 16] = spread.astype(jnp.bfloat16)
    th[pl.ds(ROWS, NMAX)] = jnp.zeros((NMAX, 16, LANES), jnp.bfloat16)
    pl.semaphore_wait(barrier, jnp.where(home, 33, 34))

    def send_own(s, n):
        where, place = ((after, 2), (before, 3), (sibling, 1))[n]
        send(v_ref.at[s], vall.at[place, s], v_send.at[3 * s + n], v_recv.at[place, s], {"row": where, "col": col})

    for s, n in ((0, 2), (0, 0), (0, 1), (1, 2)):
        send_own(s, n)
    theta_in.wait()
    v_in.wait()

    state = lax.broadcasted_iota(jnp.int32, (256, 256), 0) % 16
    state = state + 16 * (lax.broadcasted_iota(jnp.int32, (256, 256), 1) // LANES)

    def compute(u):
        place, s = ORDER[u]
        slot = places[place] * 2 + s
        if place:
            arrived(vall.at[place, s], v_recv.at[place, s])
            if place in (2, 3, 6):
                share = {2: 4, 3: 5, 6: 7}[place]
                if place == 2 and s == 0:
                    send(vall.at[2, 0], vall.at[6, 0], v_send.at[6], v_recv.at[6, 0], {"row": after, "col": col})
                if place == 3 and s == 1:
                    send(vall.at[3, 1], vall.at[6, 1], v_send.at[7], v_recv.at[6, 1], {"row": before, "col": col})
                n = 8 + 2 * (2, 3, 6).index(place) + s
                send(vall.at[place, s], vall.at[share, s], v_send.at[n], v_recv.at[share, s], {"row": sibling, "col": col})
        sector = sector_ref[slot]
        start = offset_ref[row, sector]
        end = jnp.where(sector == 15, ROWS, offset_ref[row, jnp.minimum(sector + 1, 15)])
        count = end - start
        for k in range(0, NMAX // 16, 2):
            both = th[pl.ds(start + 16 * k, 32)].reshape(512, LANES)
            both = jnp.concatenate([both[:256], both[256:]], axis=1)
            gated = jnp.dot(bd[...], both, preferred_element_type=jnp.float32)
            gated = jnp.where(state + 16 * k < count, gated, 0.0).astype(jnp.bfloat16)
            for a in range(SITES):
                for b in range(SITES):
                    for m in range(2):
                        ap[a * NMAX + 16 * (k + m): a * NMAX + 16 * (k + m + 1), b * LANES:(b + 1) * LANES] = gated[
                            (a * 4 + b) * 16:(a * 4 + b + 1) * 16, m * LANES:(m + 1) * LANES]
        product = jnp.dot(ap[...], vall[place, s], preferred_element_type=jnp.float32).astype(jnp.bfloat16)
        for a in range(SITES):
            part[u, a] = product[a * NMAX:(a + 1) * NMAX]
        axis = u % 2
        mine = z if axis == 0 else y
        far = (mine + 2) % 4
        send(part.at[u, far, pl.ds(0, HALF)], half_in.at[u, 0], half_send.at[u, 0], half_recv.at[u, 0], along(axis, 1))
        send(part.at[u, far, pl.ds(HALF, HALF)], half_in.at[u, 1], half_send.at[u, 1], half_recv.at[u, 1], along(axis, 3))

    def pass_on(u):
        axis = u % 2
        mine = z if axis == 0 else y
        for n, step in ((0, 1), (1, 3)):
            arrived(half_in.at[u, n], half_recv.at[u, n])
            to = (mine + step) % 4
            rows = pl.ds(n * HALF, HALF)
            total = part[u, to, rows, :].astype(jnp.float32) + half_in[u, n].astype(jnp.float32)
            part[u, to, rows, :] = total.astype(jnp.bfloat16)
            send(part.at[u, to], ring_in.at[u, n], ring_send.at[u, n], ring_recv.at[u, n], along(axis, step))

    def split(u):
        axis = u % 2
        mine = z if axis == 0 else y
        second = y if axis == 0 else z
        for n in range(2):
            arrived(ring_in.at[u, n], ring_recv.at[u, n])
        total = part[u, mine].astype(jnp.float32) + ring_in[u, 0].astype(jnp.float32) + ring_in[u, 1].astype(jnp.float32)
        total = total.astype(jnp.bfloat16)
        for q in range(4):
            quart[u, q] = total[:, q * LANES:(q + 1) * LANES]
        for d in (2, 1, 3):
            send(quart.at[u, (second + d) % 4], quart_in.at[u, d - 1], quart_send.at[u, d - 1],
                 quart_recv.at[u, d - 1], along(1 - axis, d))

    def finish(u):
        axis = u % 2
        place, s = ORDER[u]
        mine = z if axis == 0 else y
        second = y if axis == 0 else z
        total = quart[u, second].astype(jnp.float32)
        for d in (1, 2, 3):
            arrived(quart_in.at[u, d - 1], quart_recv.at[u, d - 1])
            total = total + quart_in[u, d - 1].astype(jnp.float32)
        done[u] = total.astype(jnp.bfloat16)
        for h in range(2):
            src = done.at[u, pl.ds(h * HALF, HALF)]
            dst = fin_ref.at[s, mine, second]
            target = 2 * row + h
            if place == 0:
                @pl.when(col == target)
                def _():
                    pltpu.make_async_copy(src, dst, fin_recv.at[s, col]).start()

                @pl.when(col != target)
                def _():
                    pltpu.make_async_remote_copy(
                        src_ref=src, dst_ref=dst, send_sem=fin_send.at[u, h], recv_sem=fin_recv.at[s, col],
                        device_id={"row": places[place], "col": target}, device_id_type=MESH).start()
            else:
                send(src, dst, fin_send.at[u, h], fin_recv.at[s, col], {"row": places[place], "col": target})

    def each(task, group):
        if 0 <= group < 4:
            for u in range(4 * group, 4 * group + 4):
                task(u)

    at_row = lax.broadcasted_iota(jnp.int32, (SHARE, KEPT), 0) + SHARE * col
    at_col = lax.broadcasted_iota(jnp.int32, (SHARE, KEPT), 1)

    def start_corr():
        for s in range(2):
            overlap(vall[0, s], corr_out.at[s], corr_diag_in.at[s], col)
            start_shared(corr_diag_in.at[s], corr_diag_send.at[s], corr_diag_recv.at[s], row, col)
            start_exchange(corr_out.at[s], corr_in.at[s], corr_send.at[s], corr_recv.at[s], row, col)

    def start_gram(s):
        @pl.loop(0, 16)
        def _(c):
            arrived(fin_ref.at[s, 0, 0], fin_recv.at[s, c])

        for a in range(SITES):
            for q in range(4):
                factor[s, a * HALF:(a + 1) * HALF, q * LANES:(q + 1) * LANES] = fin_ref[s, a, q]
        overlap(factor[s], gram_out.at[s], gram_diag_in.at[s], col)
        start_shared(gram_diag_in.at[s], gram_diag_send.at[s], gram_diag_recv.at[s], row, col)
        start_exchange(gram_out.at[s], gram_in.at[s], gram_send.at[s], gram_recv.at[s], row, col)

    def refine(s):
        correlation = finish_exchange(corr_out.at[s], corr_in.at[s], corr_send.at[s], corr_recv.at[s], col)
        corr_diag = finish_shared(corr_diag_in.at[s], corr_diag_send.at[s], corr_diag_recv.at[s], col)
        gram_diag = finish_shared(gram_diag_in.at[s], gram_diag_send.at[s], gram_diag_recv.at[s], col)
        lambdas = gram_diag / (corr_diag + 1e-06)
        gram = finish_exchange(gram_out.at[s], gram_in.at[s], gram_send.at[s], gram_recv.at[s], col)
        kept = kept_ref[sector_ref[2 * row + s]]
        across = jnp.concatenate([lambdas[q:q + 1] for q in range(4)], axis=1)
        norms = jnp.concatenate([corr_diag[q:q + 1] for q in range(4)], axis=1)
        across = jnp.broadcast_to(across, (SHARE, KEPT))
        down = jnp.sum(jnp.where(at_row == at_col, across, 0.0), axis=1, keepdims=True)
        differ = across - down
        mean = DAMPING * (across + down)
        divisor = differ * differ + mean * mean + 1e-06
        offdiag = (gram - across * correlation) * differ / divisor
        result = jnp.where(at_row == at_col, 0.5 * (1.0 - norms), offdiag)
        result = jnp.where((at_row < kept) & (at_col < kept), result, 0.0)
        out_ref[s, col] = result.astype(jnp.bfloat16)
        start_shared(out_ref.at[s], out_send.at[s], out_recv.at[s], row, col)

    each(compute, 0)
    start_corr()
    each(pass_on, 0)
    send_own(1, 1)
    each(compute, 1)
    each(split, 0)
    send_own(1, 0)
    each(pass_on, 1)
    each(finish, 0)
    each(compute, 2)
    each(split, 1)
    each(pass_on, 2)
    each(finish, 1)
    each(split, 2)
    each(compute, 3)
    each(finish, 2)
    each(pass_on, 3)
    start_gram(0)
    each(split, 3)
    each(finish, 3)
    refine(0)
    start_gram(1)
    refine(1)
    for s in range(2):
        @pl.loop(1, 16)
        def _(d):
            source = (col + d) % 16
            wait_on(out_ref.at[s, source], out_recv.at[s, source])
            wait_on(out_ref.at[s, col], out_send.at[s, source])

    for copy in sends:
        copy.wait_send()
    for s in range(2):
        for h in range(2):
            @pl.when(col != 2 * row + h)
            def _():
                pltpu.make_async_copy(done.at[s, pl.ds(h * HALF, HALF)], done.at[s, pl.ds(h * HALF, HALF)], fin_send.at[2 * s, h]).wait()


def project(theta, gate, vectors, slot_sector, block_offsets, kept):
    bf = jnp.bfloat16
    dma = pltpu.SemaphoreType.DMA
    vmem = pl.BlockSpec(memory_space=pltpu.VMEM)
    smem = pl.BlockSpec(memory_space=pltpu.SMEM)
    hbm = pl.BlockSpec(memory_space=pl.ANY)
    return pl.pallas_call(
        project_kernel,
        out_shape=(
            jax.ShapeDtypeStruct((2, SITES, 4, HALF, LANES), bf),
            jax.ShapeDtypeStruct((2, 16, SHARE, KEPT), bf),
        ),
        in_specs=[hbm, vmem, hbm, smem, smem, smem],
        out_specs=(vmem, vmem),
        scratch_shapes=[
            pltpu.VMEM((2, 16, SHARE, KEPT), bf),
            pltpu.VMEM((2, 16, SHARE, KEPT), bf),
            pltpu.VMEM((2, 16, 8, LANES), jnp.float32),
            pltpu.VMEM((2, SITES * HALF, KEPT), bf),
            pltpu.VMEM((2, 16, SHARE, KEPT), bf),
            pltpu.VMEM((2, 16, SHARE, KEPT), bf),
            pltpu.VMEM((2, 16, 8, LANES), jnp.float32),
            pltpu.VMEM((ROWS + NMAX, 16, LANES), bf),
            pltpu.VMEM((256, 256), bf),
            pltpu.VMEM((SITES * NMAX, KEPT), bf),
            pltpu.VMEM((8, 2, KEPT, KEPT), bf),
            pltpu.VMEM((UNITS, SITES, NMAX, KEPT), bf),
            pltpu.VMEM((UNITS, 2, HALF, KEPT), bf),
            pltpu.VMEM((UNITS, 2, NMAX, KEPT), bf),
            pltpu.VMEM((UNITS, 4, NMAX, LANES), bf),
            pltpu.VMEM((UNITS, 3, NMAX, LANES), bf),
            pltpu.VMEM((UNITS, NMAX, LANES), bf),
            dma, dma, dma((14,)), dma((8, 2)),
            dma((UNITS, 2)), dma((UNITS, 2)), dma((UNITS, 2)), dma((UNITS, 2)),
            dma((UNITS, 3)), dma((UNITS, 3)), dma((UNITS, 2)), dma((2, 16)),
        ] + [dma((2, 16))] * 10,
        compiler_params=pltpu.CompilerParams(has_side_effects=True, collective_id=0, vmem_limit_bytes=56 * 2**20),
        cost_estimate=pl.CostEstimate(flops=5_000_000_000, bytes_accessed=6_000_000, transcendentals=0),
        name="project",
    )(theta, gate, vectors, slot_sector, block_offsets, kept)


def final_kernel(sector_ref, kept_ref, v_ref, corr_ref, fin_ref, left_ref, right_ref):
    s = pl.program_id(0)
    kept = kept_ref[sector_ref[2 * lax.axis_index("row") + s]]
    corr_b = corr_ref[0].reshape(KEPT, KEPT)

    def keep(values):
        return jnp.where(lax.broadcasted_iota(jnp.int32, values.shape, 1) < kept, values, 0.0)

    for n in range(0, KEPT, 256):
        block = v_ref[0, n:n + 256]
        change = jnp.dot(block, corr_b, preferred_element_type=jnp.float32)
        right_ref[0, n:n + 256] = keep(block.astype(jnp.float32) + change)
    for a in range(SITES):
        block = jnp.concatenate([fin_ref[0, a, q] for q in range(4)], axis=1)
        change = jnp.dot(block, corr_b, preferred_element_type=jnp.float32)
        left_ref[:, 0, a, :] = keep(block.astype(jnp.float32) + change)


def final(slot_sector, kept, vectors, corr_b, fin):
    smem = pl.BlockSpec(memory_space=pltpu.SMEM)
    return pl.pallas_call(
        final_kernel,
        grid=(2,),
        out_shape=(
            jax.ShapeDtypeStruct((HALF, 2, SITES, KEPT), jnp.float32),
            jax.ShapeDtypeStruct((2, KEPT, KEPT), jnp.float32),
        ),
        in_specs=[
            smem, smem,
            pl.BlockSpec((1, KEPT, KEPT), lambda s: (s, 0, 0)),
            pl.BlockSpec((1, 16, SHARE, KEPT), lambda s: (s, 0, 0, 0)),
            pl.BlockSpec((1, SITES, 4, HALF, LANES), lambda s: (s, 0, 0, 0, 0)),
        ],
        out_specs=(
            pl.BlockSpec((HALF, 1, SITES, KEPT), lambda s: (0, s, 0, 0)),
            pl.BlockSpec((1, KEPT, KEPT), lambda s: (s, 0, 0)),
        ),
        compiler_params=pltpu.CompilerParams(vmem_limit_bytes=32 * 2**20),
        cost_estimate=pl.CostEstimate(flops=800_000_000, bytes_accessed=5_500_000, transcendentals=0),
        name="final",
    )(slot_sector, kept, vectors, corr_b, fin)


def shards(theta, gate, warm_start, slot_sector, kept, block_offsets):
    vectors = warm_start.reshape(2, KEPT, KEPT)
    fin, corr_b = project(theta.reshape(ROWS, 16, LANES), gate, vectors, slot_sector, block_offsets, kept)
    left, right = final(slot_sector, kept, vectors, corr_b, fin)
    return left, right.reshape(2, 4, LANES, KEPT)


def solution(mesh):
    in_specs = (P("row", None, None, "col"), P(), P("row", None, "col", None), P(), P(), P())
    out_specs = (P("col", "row", None, None), P("row", None, "col", None))
    return jax.shard_map(shards, mesh=mesh, in_specs=in_specs, out_specs=out_specs, check_vma=False)
```

```python
import jax
import jax.numpy as jnp
from jax import lax
from jax.experimental import pallas as pl
from jax.experimental.pallas import tpu as pltpu
from jax.sharding import PartitionSpec as P

NMAX = 96
HALF = NMAX // 2
SITES = 4
LANES = 128
SHARE = 32
KEPT = 512
ROWS = 1024
DAMPING = 0.25
MESH = pl.DeviceIdType.MESH

ORDER = (
    (0, 0), (1, 0), (0, 1), (1, 1),
    (2, 0), (3, 0), (4, 0), (5, 0),
    (6, 0), (7, 0), (3, 1), (5, 1),
    (2, 1), (6, 1), (4, 1), (7, 1),
)
UNITS = len(ORDER)


def overlap(block, out, diag, first, col):
    product = lax.dot_general(block, block, (((0,), (0,)), ((), ())), preferred_element_type=jnp.float32)
    product = product.astype(jnp.bfloat16)
    for c in range(16):
        out[c] = product[c * SHARE:(c + 1) * SHARE]
    wide = block.astype(jnp.float32)
    squares = jnp.sum(wide * wide, axis=0, keepdims=True)
    for q in range(4):
        diag[col, first + q:first + q + 1] = squares[:, q * LANES:(q + 1) * LANES]


def start_exchange(out, into, send_sem, recv_sem, row, col):
    @pl.loop(1, 16)
    def _(d):
        to = (col + d) % 16
        pltpu.make_async_remote_copy(
            src_ref=out.at[to], dst_ref=into.at[col], send_sem=send_sem.at[to], recv_sem=recv_sem.at[col],
            device_id={"row": row, "col": to}, device_id_type=MESH).start()


def start_shared(both, send_sem, recv_sem, row, col):
    @pl.loop(1, 16)
    def _(d):
        to = (col + d) % 16
        pltpu.make_async_remote_copy(
            src_ref=both.at[col], dst_ref=both.at[col], send_sem=send_sem.at[to], recv_sem=recv_sem.at[col],
            device_id={"row": row, "col": to}, device_id_type=MESH).start()


def wait_on(ref, sem):
    pltpu.make_async_copy(ref, ref, sem).wait()


def finish_exchange(out, into, send_sem, recv_sem, col):
    @pl.loop(1, 16)
    def _(d):
        source = (col + d) % 16
        wait_on(into.at[source], recv_sem.at[source])
        wait_on(out.at[source], send_sem.at[source])

    into[col] = out[col]
    total = into[0].astype(jnp.float32)
    for c in range(1, 16):
        total = total + into[c].astype(jnp.float32)
    return total


def finish_shared(both, send_sem, recv_sem, col):
    @pl.loop(1, 16)
    def _(d):
        source = (col + d) % 16
        wait_on(both.at[source], recv_sem.at[source])
        wait_on(both.at[col], send_sem.at[source])

    return jnp.sum(both[...], axis=0)


def project_kernel(
    theta_ref, gate_ref, v_ref, sector_ref, offset_ref, kept_ref, fin_ref, out_ref,
    corr_out, corr_in, factor, gram_out, gram_in, diag_in, th, bd, ap, vall, part, half_in, ring_in, quart, quart_in, done,
    th_sem, v_sem, v_send, v_recv, half_send, half_recv, ring_send, ring_recv,
    quart_send, quart_recv, fin_send, fin_recv, corr_send, corr_recv,
    gram_send, gram_recv, diag_send, diag_recv, out_send, out_recv,
):
    row, col = lax.axis_index("row"), lax.axis_index("col")
    x, core = row // 2, row % 2
    y, z = col // 4, col % 4
    other = 1 - core

    def rows_at(step, which):
        return ((x + step) % 4) * 2 + which

    places = (
        row, rows_at(0, other), rows_at(3, core), rows_at(1, core),
        rows_at(3, other), rows_at(1, other), rows_at(2, core), rows_at(2, other),
    )
    sibling, before, after = places[1], places[2], places[3]

    def along(axis, step):
        if axis == 0:
            return {"row": row, "col": y * 4 + (z + step) % 4}
        return {"row": row, "col": ((y + step) % 4) * 4 + z}

    sends = []

    def send(src, dst, send_sem, recv_sem, where):
        copy = pltpu.make_async_remote_copy(
            src_ref=src, dst_ref=dst, send_sem=send_sem, recv_sem=recv_sem,
            device_id=where, device_id_type=MESH,
        )
        copy.start()
        sends.append(copy)

    def arrived(dst, sem):
        pltpu.make_async_copy(dst, dst, sem).wait()

    barrier = pltpu.get_barrier_semaphore()

    def greet(where):
        pl.semaphore_signal(barrier, inc=1, device_id=where, device_id_type=MESH)

    for where in (sibling, before, after):
        greet({"row": where, "col": col})

    @pl.loop(1, 16)
    def _(d):
        greet({"row": row, "col": (col + d) % 16})

    @pl.loop(1, 16)
    def _(d):
        greet({"row": col // 2, "col": (col + d) % 16})

    home = col // 2 == row

    @pl.when(jnp.logical_not(home))
    def _():
        greet({"row": col // 2, "col": col})

    theta_in = pltpu.make_async_copy(theta_ref, th.at[pl.ds(0, ROWS)], th_sem)
    theta_in.start()
    v_in = pltpu.make_async_copy(v_ref, vall.at[0], v_sem)
    v_in.start()

    pair_r = lax.broadcasted_iota(jnp.int32, (4, 256), 0)
    pair_c = lax.broadcasted_iota(jnp.int32, (4, 256), 1)
    second_in = (pair_r == pair_c % 4).astype(jnp.bfloat16)
    same = lax.broadcasted_iota(jnp.int32, (16, 256), 0) == lax.broadcasted_iota(jnp.int32, (16, 256), 1) // 16
    for a in range(4):
        for b in range(4):
            spread = jnp.dot(gate_ref[a, b], second_in, preferred_element_type=jnp.float32)
            spread = jnp.sum(jnp.where(pair_r == pair_c // 4 % 4, spread, 0.0), axis=0, keepdims=True)
            spread = jnp.where(same, jnp.broadcast_to(spread, (16, 256)), 0.0)
            bd[(a * 4 + b) * 16:(a * 4 + b + 1) * 16] = spread.astype(jnp.bfloat16)
    th[pl.ds(ROWS, NMAX)] = jnp.zeros((NMAX, 16, LANES), jnp.bfloat16)
    pl.semaphore_wait(barrier, jnp.where(home, 33, 34))

    def send_own(s, n):
        where, place = ((after, 2), (before, 3), (sibling, 1))[n]
        send(v_ref.at[s], vall.at[place, s], v_send.at[3 * s + n], v_recv.at[place, s], {"row": where, "col": col})

    for s, n in ((0, 2), (0, 0), (0, 1), (1, 2)):
        send_own(s, n)
    theta_in.wait()
    v_in.wait()

    state = lax.broadcasted_iota(jnp.int32, (256, 256), 0) % 16
    state = state + 16 * (lax.broadcasted_iota(jnp.int32, (256, 256), 1) // LANES)

    def compute(u):
        place, s = ORDER[u]
        slot = places[place] * 2 + s
        if place:
            arrived(vall.at[place, s], v_recv.at[place, s])
            if place in (2, 3, 6):
                share = {2: 4, 3: 5, 6: 7}[place]
                if place == 2 and s == 0:
                    send(vall.at[2, 0], vall.at[6, 0], v_send.at[6], v_recv.at[6, 0], {"row": after, "col": col})
                if place == 3 and s == 1:
                    send(vall.at[3, 1], vall.at[6, 1], v_send.at[7], v_recv.at[6, 1], {"row": before, "col": col})
                n = 8 + 2 * (2, 3, 6).index(place) + s
                send(vall.at[place, s], vall.at[share, s], v_send.at[n], v_recv.at[share, s], {"row": sibling, "col": col})
        sector = sector_ref[slot]
        start = offset_ref[row, sector]
        end = jnp.where(sector == 15, ROWS, offset_ref[row, jnp.minimum(sector + 1, 15)])
        count = end - start
        for k in range(0, NMAX // 16, 2):
            both = th[pl.ds(start + 16 * k, 32)].reshape(512, LANES)
            both = jnp.concatenate([both[:256], both[256:]], axis=1)
            gated = jnp.dot(bd[...], both, preferred_element_type=jnp.float32)
            gated = jnp.where(state + 16 * k < count, gated, 0.0).astype(jnp.bfloat16)
            for a in range(SITES):
                for b in range(SITES):
                    for m in range(2):
                        ap[a * NMAX + 16 * (k + m): a * NMAX + 16 * (k + m + 1), b * LANES:(b + 1) * LANES] = gated[
                            (a * 4 + b) * 16:(a * 4 + b + 1) * 16, m * LANES:(m + 1) * LANES]
        product = jnp.dot(ap[...], vall[place, s], preferred_element_type=jnp.float32).astype(jnp.bfloat16)
        for a in range(SITES):
            part[u, a] = product[a * NMAX:(a + 1) * NMAX]
        axis = u % 2
        mine = z if axis == 0 else y
        far = (mine + 2) % 4
        send(part.at[u, far, pl.ds(0, HALF)], half_in.at[u, 0], half_send.at[u, 0], half_recv.at[u, 0], along(axis, 1))
        send(part.at[u, far, pl.ds(HALF, HALF)], half_in.at[u, 1], half_send.at[u, 1], half_recv.at[u, 1], along(axis, 3))

    def pass_on(u):
        axis = u % 2
        mine = z if axis == 0 else y
        for n, step in ((0, 1), (1, 3)):
            arrived(half_in.at[u, n], half_recv.at[u, n])
            to = (mine + step) % 4
            rows = pl.ds(n * HALF, HALF)
            total = part[u, to, rows, :].astype(jnp.float32) + half_in[u, n].astype(jnp.float32)
            part[u, to, rows, :] = total.astype(jnp.bfloat16)
            send(part.at[u, to], ring_in.at[u, n], ring_send.at[u, n], ring_recv.at[u, n], along(axis, step))

    def split(u):
        axis = u % 2
        mine = z if axis == 0 else y
        second = y if axis == 0 else z
        for n in range(2):
            arrived(ring_in.at[u, n], ring_recv.at[u, n])
        total = part[u, mine].astype(jnp.float32) + ring_in[u, 0].astype(jnp.float32) + ring_in[u, 1].astype(jnp.float32)
        total = total.astype(jnp.bfloat16)
        for q in range(4):
            quart[u, q] = total[:, q * LANES:(q + 1) * LANES]
        for d in (2, 1, 3):
            send(quart.at[u, (second + d) % 4], quart_in.at[u, d - 1], quart_send.at[u, d - 1],
                 quart_recv.at[u, d - 1], along(1 - axis, d))

    def finish(u):
        axis = u % 2
        place, s = ORDER[u]
        mine = z if axis == 0 else y
        second = y if axis == 0 else z
        total = quart[u, second].astype(jnp.float32)
        for d in (1, 2, 3):
            arrived(quart_in.at[u, d - 1], quart_recv.at[u, d - 1])
            total = total + quart_in[u, d - 1].astype(jnp.float32)
        done[u] = total.astype(jnp.bfloat16)
        for h in range(2):
            src = done.at[u, pl.ds(h * HALF, HALF)]
            dst = fin_ref.at[s, mine, second]
            target = 2 * row + h
            if place == 0:
                @pl.when(col == target)
                def _():
                    pltpu.make_async_copy(src, dst, fin_recv.at[s, col]).start()

                @pl.when(col != target)
                def _():
                    pltpu.make_async_remote_copy(
                        src_ref=src, dst_ref=dst, send_sem=fin_send.at[u, h], recv_sem=fin_recv.at[s, col],
                        device_id={"row": places[place], "col": target}, device_id_type=MESH).start()
            else:
                send(src, dst, fin_send.at[u, h], fin_recv.at[s, col], {"row": places[place], "col": target})

    def each(task, group):
        if 0 <= group < 4:
            for u in range(4 * group, 4 * group + 4):
                task(u)

    at_row = lax.broadcasted_iota(jnp.int32, (SHARE, KEPT), 0) + SHARE * col
    at_col = lax.broadcasted_iota(jnp.int32, (SHARE, KEPT), 1)

    def start_corr():
        for s in range(2):
            overlap(vall[0, s], corr_out.at[s], diag_in.at[s], 4, col)
            start_exchange(corr_out.at[s], corr_in.at[s], corr_send.at[s], corr_recv.at[s], row, col)

    def start_gram(s):
        @pl.loop(0, 16)
        def _(c):
            arrived(fin_ref.at[s, 0, 0], fin_recv.at[s, c])

        for a in range(SITES):
            for q in range(4):
                factor[s, a * HALF:(a + 1) * HALF, q * LANES:(q + 1) * LANES] = fin_ref[s, a, q]
        overlap(factor[s], gram_out.at[s], diag_in.at[s], 0, col)
        start_shared(diag_in.at[s], diag_send.at[s], diag_recv.at[s], row, col)
        start_exchange(gram_out.at[s], gram_in.at[s], gram_send.at[s], gram_recv.at[s], row, col)

    def refine(s):
        correlation = finish_exchange(corr_out.at[s], corr_in.at[s], corr_send.at[s], corr_recv.at[s], col)
        diags = finish_shared(diag_in.at[s], diag_send.at[s], diag_recv.at[s], col)
        corr_diag = diags[4:]
        lambdas = diags[:4] / (corr_diag + 1e-06)
        gram = finish_exchange(gram_out.at[s], gram_in.at[s], gram_send.at[s], gram_recv.at[s], col)
        kept = kept_ref[sector_ref[2 * row + s]]
        across = jnp.concatenate([lambdas[q:q + 1] for q in range(4)], axis=1)
        norms = jnp.concatenate([corr_diag[q:q + 1] for q in range(4)], axis=1)
        across = jnp.broadcast_to(across, (SHARE, KEPT))
        down = jnp.sum(jnp.where(at_row == at_col, across, 0.0), axis=1, keepdims=True)
        differ = across - down
        mean = DAMPING * (across + down)
        divisor = differ * differ + mean * mean + 1e-06
        offdiag = (gram - across * correlation) * differ / divisor
        result = jnp.where(at_row == at_col, 0.5 * (1.0 - norms), offdiag)
        result = jnp.where((at_row < kept) & (at_col < kept), result, 0.0)
        out_ref[s, col] = result.astype(jnp.bfloat16)
        start_shared(out_ref.at[s], out_send.at[s], out_recv.at[s], row, col)

    each(compute, 0)
    start_corr()
    each(pass_on, 0)
    send_own(1, 1)
    each(compute, 1)
    each(split, 0)
    send_own(1, 0)
    each(pass_on, 1)
    each(finish, 0)
    each(compute, 2)
    each(split, 1)
    each(pass_on, 2)
    each(finish, 1)
    each(split, 2)
    each(compute, 3)
    each(finish, 2)
    each(pass_on, 3)
    start_gram(0)
    each(split, 3)
    each(finish, 3)
    refine(0)
    start_gram(1)
    refine(1)
    for s in range(2):
        @pl.loop(1, 16)
        def _(d):
            source = (col + d) % 16
            wait_on(out_ref.at[s, source], out_recv.at[s, source])
            wait_on(out_ref.at[s, col], out_send.at[s, source])

    for copy in sends:
        copy.wait_send()
    for s in range(2):
        for h in range(2):
            @pl.when(col != 2 * row + h)
            def _():
                pltpu.make_async_copy(done.at[s, pl.ds(h * HALF, HALF)], done.at[s, pl.ds(h * HALF, HALF)], fin_send.at[2 * s, h]).wait()


def project(theta, gate, vectors, slot_sector, block_offsets, kept):
    bf = jnp.bfloat16
    dma = pltpu.SemaphoreType.DMA
    vmem = pl.BlockSpec(memory_space=pltpu.VMEM)
    smem = pl.BlockSpec(memory_space=pltpu.SMEM)
    hbm = pl.BlockSpec(memory_space=pl.ANY)
    return pl.pallas_call(
        project_kernel,
        out_shape=(
            jax.ShapeDtypeStruct((2, SITES, 4, HALF, LANES), bf),
            jax.ShapeDtypeStruct((2, 16, SHARE, KEPT), bf),
        ),
        in_specs=[hbm, vmem, hbm, smem, smem, smem],
        out_specs=(vmem, vmem),
        scratch_shapes=[
            pltpu.VMEM((2, 16, SHARE, KEPT), bf),
            pltpu.VMEM((2, 16, SHARE, KEPT), bf),
            pltpu.VMEM((2, SITES * HALF, KEPT), bf),
            pltpu.VMEM((2, 16, SHARE, KEPT), bf),
            pltpu.VMEM((2, 16, SHARE, KEPT), bf),
            pltpu.VMEM((2, 16, 8, LANES), jnp.float32),
            pltpu.VMEM((ROWS + NMAX, 16, LANES), bf),
            pltpu.VMEM((256, 256), bf),
            pltpu.VMEM((SITES * NMAX, KEPT), bf),
            pltpu.VMEM((8, 2, KEPT, KEPT), bf),
            pltpu.VMEM((UNITS, SITES, NMAX, KEPT), bf),
            pltpu.VMEM((UNITS, 2, HALF, KEPT), bf),
            pltpu.VMEM((UNITS, 2, NMAX, KEPT), bf),
            pltpu.VMEM((UNITS, 4, NMAX, LANES), bf),
            pltpu.VMEM((UNITS, 3, NMAX, LANES), bf),
            pltpu.VMEM((UNITS, NMAX, LANES), bf),
            dma, dma, dma((14,)), dma((8, 2)),
            dma((UNITS, 2)), dma((UNITS, 2)), dma((UNITS, 2)), dma((UNITS, 2)),
            dma((UNITS, 3)), dma((UNITS, 3)), dma((UNITS, 2)), dma((2, 16)),
        ] + [dma((2, 16))] * 8,
        compiler_params=pltpu.CompilerParams(has_side_effects=True, collective_id=0, vmem_limit_bytes=56 * 2**20),
        cost_estimate=pl.CostEstimate(flops=5_000_000_000, bytes_accessed=6_000_000, transcendentals=0),
        name="project",
    )(theta, gate, vectors, slot_sector, block_offsets, kept)


def final_kernel(sector_ref, kept_ref, v_ref, corr_ref, fin_ref, left_ref, right_ref):
    s = pl.program_id(0)
    kept = kept_ref[sector_ref[2 * lax.axis_index("row") + s]]
    corr_b = corr_ref[0].reshape(KEPT, KEPT)

    def keep(values):
        return jnp.where(lax.broadcasted_iota(jnp.int32, values.shape, 1) < kept, values, 0.0)

    for n in range(0, KEPT, 256):
        block = v_ref[0, n:n + 256]
        change = jnp.dot(block, corr_b, preferred_element_type=jnp.float32)
        right_ref[0, n:n + 256] = keep(block.astype(jnp.float32) + change)
    for a in range(SITES):
        block = jnp.concatenate([fin_ref[0, a, q] for q in range(4)], axis=1)
        change = jnp.dot(block, corr_b, preferred_element_type=jnp.float32)
        left_ref[:, 0, a, :] = keep(block.astype(jnp.float32) + change)


def final(slot_sector, kept, vectors, corr_b, fin):
    smem = pl.BlockSpec(memory_space=pltpu.SMEM)
    return pl.pallas_call(
        final_kernel,
        grid=(2,),
        out_shape=(
            jax.ShapeDtypeStruct((HALF, 2, SITES, KEPT), jnp.float32),
            jax.ShapeDtypeStruct((2, KEPT, KEPT), jnp.float32),
        ),
        in_specs=[
            smem, smem,
            pl.BlockSpec((1, KEPT, KEPT), lambda s: (s, 0, 0)),
            pl.BlockSpec((1, 16, SHARE, KEPT), lambda s: (s, 0, 0, 0)),
            pl.BlockSpec((1, SITES, 4, HALF, LANES), lambda s: (s, 0, 0, 0, 0)),
        ],
        out_specs=(
            pl.BlockSpec((HALF, 1, SITES, KEPT), lambda s: (0, s, 0, 0)),
            pl.BlockSpec((1, KEPT, KEPT), lambda s: (s, 0, 0)),
        ),
        compiler_params=pltpu.CompilerParams(vmem_limit_bytes=32 * 2**20),
        cost_estimate=pl.CostEstimate(flops=800_000_000, bytes_accessed=5_500_000, transcendentals=0),
        name="final",
    )(slot_sector, kept, vectors, corr_b, fin)


def shards(theta, gate, warm_start, slot_sector, kept, block_offsets):
    vectors = warm_start.reshape(2, KEPT, KEPT)
    fin, corr_b = project(theta.reshape(ROWS, 16, LANES), gate, vectors, slot_sector, block_offsets, kept)
    left, right = final(slot_sector, kept, vectors, corr_b, fin)
    return left, right.reshape(2, 4, LANES, KEPT)


def solution(mesh):
    in_specs = (P("row", None, None, "col"), P(), P("row", None, "col", None), P(), P(), P())
    out_specs = (P("col", "row", None, None), P("row", None, "col", None))
    return jax.shard_map(shards, mesh=mesh, in_specs=in_specs, out_specs=out_specs, check_vma=False)
```

```python
import jax
import jax.numpy as jnp
from jax import lax
from jax.experimental import pallas as pl
from jax.experimental.pallas import tpu as pltpu
from jax.sharding import PartitionSpec as P

NMAX = 96
HALF = NMAX // 2
SITES = 4
LANES = 128
SHARE = 32
KEPT = 512
ROWS = 1024
DAMPING = 0.25
MESH = pl.DeviceIdType.MESH

ORDER = (
    (0, 0), (1, 0), (0, 1), (1, 1),
    (2, 0), (3, 0), (4, 0), (5, 0),
    (6, 0), (7, 0), (3, 1), (5, 1),
    (2, 1), (6, 1), (4, 1), (7, 1),
)
UNITS = len(ORDER)


def overlap(block, out, diag, first, col):
    product = lax.dot_general(block, block, (((0,), (0,)), ((), ())), preferred_element_type=jnp.float32)
    product = product.astype(jnp.bfloat16)
    for c in range(16):
        out[c] = product[c * SHARE:(c + 1) * SHARE]
    wide = block.astype(jnp.float32)
    squares = jnp.sum(wide * wide, axis=0, keepdims=True)
    for q in range(4):
        diag[col, first + q:first + q + 1] = squares[:, q * LANES:(q + 1) * LANES]


def start_exchange(out, into, send_sem, recv_sem, row, col):
    @pl.loop(1, 16)
    def _(d):
        to = (col + d) % 16
        pltpu.make_async_remote_copy(
            src_ref=out.at[to], dst_ref=into.at[col], send_sem=send_sem.at[to], recv_sem=recv_sem.at[col],
            device_id={"row": row, "col": to}, device_id_type=MESH).start()


def start_shared(both, send_sem, recv_sem, row, col):
    @pl.loop(1, 16)
    def _(d):
        to = (col + d) % 16
        pltpu.make_async_remote_copy(
            src_ref=both.at[col], dst_ref=both.at[col], send_sem=send_sem.at[to], recv_sem=recv_sem.at[col],
            device_id={"row": row, "col": to}, device_id_type=MESH).start()


def wait_on(ref, sem):
    pltpu.make_async_copy(ref, ref, sem).wait()


def finish_exchange(out, into, send_sem, recv_sem, col):
    @pl.loop(1, 16)
    def _(d):
        source = (col + d) % 16
        wait_on(into.at[source], recv_sem.at[source])

    into[col] = out[col]
    total = into[0].astype(jnp.float32)
    for c in range(1, 16):
        total = total + into[c].astype(jnp.float32)
    return total


def finish_shared(both, send_sem, recv_sem, col):
    @pl.loop(1, 16)
    def _(d):
        source = (col + d) % 16
        wait_on(both.at[source], recv_sem.at[source])

    return jnp.sum(both[...], axis=0)


def project_kernel(
    theta_ref, gate_ref, v_ref, sector_ref, offset_ref, kept_ref, fin_ref, out_ref,
    corr_out, corr_in, factor, gram_out, gram_in, diag_in, th, bd, ap, vall, part, half_in, ring_in, quart, quart_in, done,
    th_sem, v_sem, v_send, v_recv, half_send, half_recv, ring_send, ring_recv,
    quart_send, quart_recv, fin_send, fin_recv, corr_send, corr_recv,
    gram_send, gram_recv, diag_send, diag_recv, out_send, out_recv,
):
    row, col = lax.axis_index("row"), lax.axis_index("col")
    x, core = row // 2, row % 2
    y, z = col // 4, col % 4
    other = 1 - core

    def rows_at(step, which):
        return ((x + step) % 4) * 2 + which

    places = (
        row, rows_at(0, other), rows_at(3, core), rows_at(1, core),
        rows_at(3, other), rows_at(1, other), rows_at(2, core), rows_at(2, other),
    )
    sibling, before, after = places[1], places[2], places[3]

    def along(axis, step):
        if axis == 0:
            return {"row": row, "col": y * 4 + (z + step) % 4}
        return {"row": row, "col": ((y + step) % 4) * 4 + z}

    sends = []

    def send(src, dst, send_sem, recv_sem, where):
        copy = pltpu.make_async_remote_copy(
            src_ref=src, dst_ref=dst, send_sem=send_sem, recv_sem=recv_sem,
            device_id=where, device_id_type=MESH,
        )
        copy.start()
        sends.append(copy)

    def arrived(dst, sem):
        pltpu.make_async_copy(dst, dst, sem).wait()

    barrier = pltpu.get_barrier_semaphore()

    def greet(where):
        pl.semaphore_signal(barrier, inc=1, device_id=where, device_id_type=MESH)

    for where in (sibling, before, after):
        greet({"row": where, "col": col})

    @pl.loop(1, 16)
    def _(d):
        greet({"row": row, "col": (col + d) % 16})

    @pl.loop(1, 16)
    def _(d):
        greet({"row": col // 2, "col": (col + d) % 16})

    home = col // 2 == row

    @pl.when(jnp.logical_not(home))
    def _():
        greet({"row": col // 2, "col": col})

    theta_in = pltpu.make_async_copy(theta_ref, th.at[pl.ds(0, ROWS)], th_sem)
    theta_in.start()
    v_in = pltpu.make_async_copy(v_ref, vall.at[0], v_sem)
    v_in.start()

    pair_r = lax.broadcasted_iota(jnp.int32, (4, 256), 0)
    pair_c = lax.broadcasted_iota(jnp.int32, (4, 256), 1)
    second_in = (pair_r == pair_c % 4).astype(jnp.bfloat16)
    same = lax.broadcasted_iota(jnp.int32, (16, 256), 0) == lax.broadcasted_iota(jnp.int32, (16, 256), 1) // 16
    for a in range(4):
        for b in range(4):
            spread = jnp.dot(gate_ref[a, b], second_in, preferred_element_type=jnp.float32)
            spread = jnp.sum(jnp.where(pair_r == pair_c // 4 % 4, spread, 0.0), axis=0, keepdims=True)
            spread = jnp.where(same, jnp.broadcast_to(spread, (16, 256)), 0.0)
            bd[(a * 4 + b) * 16:(a * 4 + b + 1) * 16] = spread.astype(jnp.bfloat16)
    th[pl.ds(ROWS, NMAX)] = jnp.zeros((NMAX, 16, LANES), jnp.bfloat16)
    pl.semaphore_wait(barrier, jnp.where(home, 33, 34))

    def send_own(s, n):
        where, place = ((after, 2), (before, 3), (sibling, 1))[n]
        send(v_ref.at[s], vall.at[place, s], v_send.at[3 * s + n], v_recv.at[place, s], {"row": where, "col": col})

    for s, n in ((0, 2), (0, 0), (0, 1), (1, 2)):
        send_own(s, n)
    theta_in.wait()
    v_in.wait()

    state = lax.broadcasted_iota(jnp.int32, (256, 256), 0) % 16
    state = state + 16 * (lax.broadcasted_iota(jnp.int32, (256, 256), 1) // LANES)

    def compute(u):
        place, s = ORDER[u]
        slot = places[place] * 2 + s
        if place:
            arrived(vall.at[place, s], v_recv.at[place, s])
            if place in (2, 3, 6):
                share = {2: 4, 3: 5, 6: 7}[place]
                if place == 2 and s == 0:
                    send(vall.at[2, 0], vall.at[6, 0], v_send.at[6], v_recv.at[6, 0], {"row": after, "col": col})
                if place == 3 and s == 1:
                    send(vall.at[3, 1], vall.at[6, 1], v_send.at[7], v_recv.at[6, 1], {"row": before, "col": col})
                n = 8 + 2 * (2, 3, 6).index(place) + s
                send(vall.at[place, s], vall.at[share, s], v_send.at[n], v_recv.at[share, s], {"row": sibling, "col": col})
        sector = sector_ref[slot]
        start = offset_ref[row, sector]
        end = jnp.where(sector == 15, ROWS, offset_ref[row, jnp.minimum(sector + 1, 15)])
        count = end - start
        for k in range(0, NMAX // 16, 2):
            both = th[pl.ds(start + 16 * k, 32)].reshape(512, LANES)
            both = jnp.concatenate([both[:256], both[256:]], axis=1)
            gated = jnp.dot(bd[...], both, preferred_element_type=jnp.float32)
            gated = jnp.where(state + 16 * k < count, gated, 0.0).astype(jnp.bfloat16)
            for a in range(SITES):
                for b in range(SITES):
                    for m in range(2):
                        ap[a * NMAX + 16 * (k + m): a * NMAX + 16 * (k + m + 1), b * LANES:(b + 1) * LANES] = gated[
                            (a * 4 + b) * 16:(a * 4 + b + 1) * 16, m * LANES:(m + 1) * LANES]
        product = jnp.dot(ap[...], vall[place, s], preferred_element_type=jnp.float32).astype(jnp.bfloat16)
        for a in range(SITES):
            part[u, a] = product[a * NMAX:(a + 1) * NMAX]
        axis = u % 2
        mine = z if axis == 0 else y
        far = (mine + 2) % 4
        send(part.at[u, far, pl.ds(0, HALF)], half_in.at[u, 0], half_send.at[u, 0], half_recv.at[u, 0], along(axis, 1))
        send(part.at[u, far, pl.ds(HALF, HALF)], half_in.at[u, 1], half_send.at[u, 1], half_recv.at[u, 1], along(axis, 3))

    def pass_on(u):
        axis = u % 2
        mine = z if axis == 0 else y
        for n, step in ((0, 1), (1, 3)):
            arrived(half_in.at[u, n], half_recv.at[u, n])
            to = (mine + step) % 4
            rows = pl.ds(n * HALF, HALF)
            total = part[u, to, rows, :].astype(jnp.float32) + half_in[u, n].astype(jnp.float32)
            part[u, to, rows, :] = total.astype(jnp.bfloat16)
            send(part.at[u, to], ring_in.at[u, n], ring_send.at[u, n], ring_recv.at[u, n], along(axis, step))

    def split(u):
        axis = u % 2
        mine = z if axis == 0 else y
        second = y if axis == 0 else z
        for n in range(2):
            arrived(ring_in.at[u, n], ring_recv.at[u, n])
        total = part[u, mine].astype(jnp.float32) + ring_in[u, 0].astype(jnp.float32) + ring_in[u, 1].astype(jnp.float32)
        total = total.astype(jnp.bfloat16)
        for q in range(4):
            quart[u, q] = total[:, q * LANES:(q + 1) * LANES]
        for d in (2, 1, 3):
            send(quart.at[u, (second + d) % 4], quart_in.at[u, d - 1], quart_send.at[u, d - 1],
                 quart_recv.at[u, d - 1], along(1 - axis, d))

    def finish(u):
        axis = u % 2
        place, s = ORDER[u]
        mine = z if axis == 0 else y
        second = y if axis == 0 else z
        total = quart[u, second].astype(jnp.float32)
        for d in (1, 2, 3):
            arrived(quart_in.at[u, d - 1], quart_recv.at[u, d - 1])
            total = total + quart_in[u, d - 1].astype(jnp.float32)
        done[u] = total.astype(jnp.bfloat16)
        for h in range(2):
            src = done.at[u, pl.ds(h * HALF, HALF)]
            dst = fin_ref.at[s, mine, second]
            target = 2 * row + h
            if place == 0:
                @pl.when(col == target)
                def _():
                    pltpu.make_async_copy(src, dst, fin_recv.at[s, col]).start()

                @pl.when(col != target)
                def _():
                    pltpu.make_async_remote_copy(
                        src_ref=src, dst_ref=dst, send_sem=fin_send.at[u, h], recv_sem=fin_recv.at[s, col],
                        device_id={"row": places[place], "col": target}, device_id_type=MESH).start()
            else:
                send(src, dst, fin_send.at[u, h], fin_recv.at[s, col], {"row": places[place], "col": target})

    def each(task, group):
        if 0 <= group < 4:
            for u in range(4 * group, 4 * group + 4):
                task(u)

    at_row = lax.broadcasted_iota(jnp.int32, (SHARE, KEPT), 0) + SHARE * col
    at_col = lax.broadcasted_iota(jnp.int32, (SHARE, KEPT), 1)

    def start_corr():
        for s in range(2):
            overlap(vall[0, s], corr_out.at[s], diag_in.at[s], 4, col)
            start_exchange(corr_out.at[s], corr_in.at[s], corr_send.at[s], corr_recv.at[s], row, col)

    def start_gram(s):
        @pl.loop(0, 16)
        def _(c):
            arrived(fin_ref.at[s, 0, 0], fin_recv.at[s, c])

        for a in range(SITES):
            for q in range(4):
                factor[s, a * HALF:(a + 1) * HALF, q * LANES:(q + 1) * LANES] = fin_ref[s, a, q]
        overlap(factor[s], gram_out.at[s], diag_in.at[s], 0, col)
        start_shared(diag_in.at[s], diag_send.at[s], diag_recv.at[s], row, col)
        start_exchange(gram_out.at[s], gram_in.at[s], gram_send.at[s], gram_recv.at[s], row, col)

    def refine(s):
        correlation = finish_exchange(corr_out.at[s], corr_in.at[s], corr_send.at[s], corr_recv.at[s], col)
        diags = finish_shared(diag_in.at[s], diag_send.at[s], diag_recv.at[s], col)
        corr_diag = diags[4:]
        lambdas = diags[:4] / (corr_diag + 1e-06)
        gram = finish_exchange(gram_out.at[s], gram_in.at[s], gram_send.at[s], gram_recv.at[s], col)
        kept = kept_ref[sector_ref[2 * row + s]]
        across = jnp.concatenate([lambdas[q:q + 1] for q in range(4)], axis=1)
        norms = jnp.concatenate([corr_diag[q:q + 1] for q in range(4)], axis=1)
        across = jnp.broadcast_to(across, (SHARE, KEPT))
        down = jnp.sum(jnp.where(at_row == at_col, across, 0.0), axis=1, keepdims=True)
        differ = across - down
        mean = DAMPING * (across + down)
        divisor = differ * differ + mean * mean + 1e-06
        offdiag = (gram - across * correlation) * differ / divisor
        result = jnp.where(at_row == at_col, 0.5 * (1.0 - norms), offdiag)
        result = jnp.where((at_row < kept) & (at_col < kept), result, 0.0)
        out_ref[s, col] = result.astype(jnp.bfloat16)
        start_shared(out_ref.at[s], out_send.at[s], out_recv.at[s], row, col)

    each(compute, 0)
    start_corr()
    each(pass_on, 0)
    send_own(1, 1)
    each(compute, 1)
    each(split, 0)
    send_own(1, 0)
    each(pass_on, 1)
    each(finish, 0)
    each(compute, 2)
    each(split, 1)
    each(pass_on, 2)
    each(finish, 1)
    each(split, 2)
    each(compute, 3)
    each(finish, 2)
    each(pass_on, 3)
    start_gram(0)
    each(split, 3)
    each(finish, 3)
    refine(0)
    start_gram(1)
    refine(1)
    for s in range(2):
        @pl.loop(1, 16)
        def _(d):
            to = (col + d) % 16
            wait_on(corr_out.at[s, to], corr_send.at[s, to])
            wait_on(gram_out.at[s, to], gram_send.at[s, to])
            wait_on(diag_in.at[s, col], diag_send.at[s, to])

    for copy in sends:
        copy.wait_send()
    for s in range(2):
        for h in range(2):
            @pl.when(col != 2 * row + h)
            def _():
                pltpu.make_async_copy(done.at[s, pl.ds(h * HALF, HALF)], done.at[s, pl.ds(h * HALF, HALF)], fin_send.at[2 * s, h]).wait()

    for s in range(2):
        @pl.loop(1, 16)
        def _(d):
            source = (col + d) % 16
            wait_on(out_ref.at[s, source], out_recv.at[s, source])
            wait_on(out_ref.at[s, col], out_send.at[s, source])


def project(theta, gate, vectors, slot_sector, block_offsets, kept):
    bf = jnp.bfloat16
    dma = pltpu.SemaphoreType.DMA
    vmem = pl.BlockSpec(memory_space=pltpu.VMEM)
    smem = pl.BlockSpec(memory_space=pltpu.SMEM)
    hbm = pl.BlockSpec(memory_space=pl.ANY)
    return pl.pallas_call(
        project_kernel,
        out_shape=(
            jax.ShapeDtypeStruct((2, SITES, 4, HALF, LANES), bf),
            jax.ShapeDtypeStruct((2, 16, SHARE, KEPT), bf),
        ),
        in_specs=[hbm, vmem, hbm, smem, smem, smem],
        out_specs=(vmem, vmem),
        scratch_shapes=[
            pltpu.VMEM((2, 16, SHARE, KEPT), bf),
            pltpu.VMEM((2, 16, SHARE, KEPT), bf),
            pltpu.VMEM((2, SITES * HALF, KEPT), bf),
            pltpu.VMEM((2, 16, SHARE, KEPT), bf),
            pltpu.VMEM((2, 16, SHARE, KEPT), bf),
            pltpu.VMEM((2, 16, 8, LANES), jnp.float32),
            pltpu.VMEM((ROWS + NMAX, 16, LANES), bf),
            pltpu.VMEM((256, 256), bf),
            pltpu.VMEM((SITES * NMAX, KEPT), bf),
            pltpu.VMEM((8, 2, KEPT, KEPT), bf),
            pltpu.VMEM((UNITS, SITES, NMAX, KEPT), bf),
            pltpu.VMEM((UNITS, 2, HALF, KEPT), bf),
            pltpu.VMEM((UNITS, 2, NMAX, KEPT), bf),
            pltpu.VMEM((UNITS, 4, NMAX, LANES), bf),
            pltpu.VMEM((UNITS, 3, NMAX, LANES), bf),
            pltpu.VMEM((UNITS, NMAX, LANES), bf),
            dma, dma, dma((14,)), dma((8, 2)),
            dma((UNITS, 2)), dma((UNITS, 2)), dma((UNITS, 2)), dma((UNITS, 2)),
            dma((UNITS, 3)), dma((UNITS, 3)), dma((UNITS, 2)), dma((2, 16)),
        ] + [dma((2, 16))] * 8,
        compiler_params=pltpu.CompilerParams(has_side_effects=True, collective_id=0, vmem_limit_bytes=56 * 2**20),
        cost_estimate=pl.CostEstimate(flops=5_000_000_000, bytes_accessed=6_000_000, transcendentals=0),
        name="project",
    )(theta, gate, vectors, slot_sector, block_offsets, kept)


def final_kernel(sector_ref, kept_ref, v_ref, corr_ref, fin_ref, left_ref, right_ref):
    s = pl.program_id(0)
    kept = kept_ref[sector_ref[2 * lax.axis_index("row") + s]]
    corr_b = corr_ref[0].reshape(KEPT, KEPT)

    def keep(values):
        return jnp.where(lax.broadcasted_iota(jnp.int32, values.shape, 1) < kept, values, 0.0)

    for n in range(0, KEPT, 256):
        block = v_ref[0, n:n + 256]
        change = jnp.dot(block, corr_b, preferred_element_type=jnp.float32)
        right_ref[0, n:n + 256] = keep(block.astype(jnp.float32) + change)
    for a in range(SITES):
        block = jnp.concatenate([fin_ref[0, a, q] for q in range(4)], axis=1)
        change = jnp.dot(block, corr_b, preferred_element_type=jnp.float32)
        left_ref[:, 0, a, :] = keep(block.astype(jnp.float32) + change)


def final(slot_sector, kept, vectors, corr_b, fin):
    smem = pl.BlockSpec(memory_space=pltpu.SMEM)
    return pl.pallas_call(
        final_kernel,
        grid=(2,),
        out_shape=(
            jax.ShapeDtypeStruct((HALF, 2, SITES, KEPT), jnp.float32),
            jax.ShapeDtypeStruct((2, KEPT, KEPT), jnp.float32),
        ),
        in_specs=[
            smem, smem,
            pl.BlockSpec((1, KEPT, KEPT), lambda s: (s, 0, 0)),
            pl.BlockSpec((1, 16, SHARE, KEPT), lambda s: (s, 0, 0, 0)),
            pl.BlockSpec((1, SITES, 4, HALF, LANES), lambda s: (s, 0, 0, 0, 0)),
        ],
        out_specs=(
            pl.BlockSpec((HALF, 1, SITES, KEPT), lambda s: (0, s, 0, 0)),
            pl.BlockSpec((1, KEPT, KEPT), lambda s: (s, 0, 0)),
        ),
        compiler_params=pltpu.CompilerParams(vmem_limit_bytes=32 * 2**20),
        cost_estimate=pl.CostEstimate(flops=800_000_000, bytes_accessed=5_500_000, transcendentals=0),
        name="final",
    )(slot_sector, kept, vectors, corr_b, fin)


def shards(theta, gate, warm_start, slot_sector, kept, block_offsets):
    vectors = warm_start.reshape(2, KEPT, KEPT)
    fin, corr_b = project(theta.reshape(ROWS, 16, LANES), gate, vectors, slot_sector, block_offsets, kept)
    left, right = final(slot_sector, kept, vectors, corr_b, fin)
    return left, right.reshape(2, 4, LANES, KEPT)


def solution(mesh):
    in_specs = (P("row", None, None, "col"), P(), P("row", None, "col", None), P(), P(), P())
    out_specs = (P("col", "row", None, None), P("row", None, "col", None))
    return jax.shard_map(shards, mesh=mesh, in_specs=in_specs, out_specs=out_specs, check_vma=False)
```

```python
import jax
import jax.numpy as jnp
from jax import lax
from jax.experimental import pallas as pl
from jax.experimental.pallas import tpu as pltpu
from jax.sharding import PartitionSpec as P

NMAX = 96
HALF = NMAX // 2
SITES = 4
LANES = 128
SHARE = 32
KEPT = 512
ROWS = 1024
DAMPING = 0.25
MESH = pl.DeviceIdType.MESH

ORDER = (
    (0, 0), (1, 0), (0, 1), (1, 1),
    (2, 0), (3, 0), (4, 0), (5, 0),
    (6, 0), (7, 0), (3, 1), (5, 1),
    (2, 1), (6, 1), (4, 1), (7, 1),
)
UNITS = len(ORDER)


def overlap(block, out, diag, first, col):
    product = lax.dot_general(block, block, (((0,), (0,)), ((), ())), preferred_element_type=jnp.float32)
    product = product.astype(jnp.bfloat16)
    for c in range(16):
        out[c] = product[c * SHARE:(c + 1) * SHARE]
    wide = block.astype(jnp.float32)
    squares = jnp.sum(wide * wide, axis=0, keepdims=True)
    for q in range(4):
        diag[col, first + q:first + q + 1] = squares[:, q * LANES:(q + 1) * LANES]


def start_exchange(out, into, send_sem, recv_sem, row, col):
    @pl.loop(1, 16)
    def _(d):
        to = (col + d) % 16
        pltpu.make_async_remote_copy(
            src_ref=out.at[to], dst_ref=into.at[col], send_sem=send_sem.at[to], recv_sem=recv_sem.at[col],
            device_id={"row": row, "col": to}, device_id_type=MESH).start()


def start_shared(both, send_sem, recv_sem, row, col):
    @pl.loop(1, 16)
    def _(d):
        to = (col + d) % 16
        pltpu.make_async_remote_copy(
            src_ref=both.at[col], dst_ref=both.at[col], send_sem=send_sem.at[to], recv_sem=recv_sem.at[col],
            device_id={"row": row, "col": to}, device_id_type=MESH).start()


def wait_on(ref, sem):
    pltpu.make_async_copy(ref, ref, sem).wait()


def finish_exchange(out, into, send_sem, recv_sem, col):
    @pl.loop(1, 16)
    def _(d):
        source = (col + d) % 16
        wait_on(into.at[source], recv_sem.at[source])
        wait_on(out.at[source], send_sem.at[source])

    into[col] = out[col]
    total = into[0].astype(jnp.float32)
    for c in range(1, 16):
        total = total + into[c].astype(jnp.float32)
    return total


def finish_shared(both, send_sem, recv_sem, col):
    @pl.loop(1, 16)
    def _(d):
        source = (col + d) % 16
        wait_on(both.at[source], recv_sem.at[source])
        wait_on(both.at[col], send_sem.at[source])

    return jnp.sum(both[...], axis=0)


def project_kernel(
    theta_ref, gate_ref, v_ref, sector_ref, offset_ref, kept_ref, fin_ref, out_ref,
    corr_out, corr_in, factor, gram_out, gram_in, diag_in, th, bd, ap, vall, part, half_in, ring_in, quart, quart_in, done,
    th_sem, v_sem, v_send, v_recv, half_send, half_recv, ring_send, ring_recv,
    quart_send, quart_recv, fin_send, fin_recv, corr_send, corr_recv,
    gram_send, gram_recv, diag_send, diag_recv, out_send, out_recv,
):
    row, col = lax.axis_index("row"), lax.axis_index("col")
    x, core = row // 2, row % 2
    y, z = col // 4, col % 4
    other = 1 - core

    def rows_at(step, which):
        return ((x + step) % 4) * 2 + which

    places = (
        row, rows_at(0, other), rows_at(3, core), rows_at(1, core),
        rows_at(3, other), rows_at(1, other), rows_at(2, core), rows_at(2, other),
    )
    sibling, before, after = places[1], places[2], places[3]

    def along(axis, step):
        if axis == 0:
            return {"row": row, "col": y * 4 + (z + step) % 4}
        return {"row": row, "col": ((y + step) % 4) * 4 + z}

    sends = []

    def send(src, dst, send_sem, recv_sem, where):
        copy = pltpu.make_async_remote_copy(
            src_ref=src, dst_ref=dst, send_sem=send_sem, recv_sem=recv_sem,
            device_id=where, device_id_type=MESH,
        )
        copy.start()
        sends.append(copy)

    def arrived(dst, sem):
        pltpu.make_async_copy(dst, dst, sem).wait()

    barrier = pltpu.get_barrier_semaphore()

    def greet(where):
        pl.semaphore_signal(barrier, inc=1, device_id=where, device_id_type=MESH)

    for where in (sibling, before, after):
        greet({"row": where, "col": col})

    @pl.loop(1, 16)
    def _(d):
        greet({"row": row, "col": (col + d) % 16})

    @pl.loop(1, 16)
    def _(d):
        greet({"row": col // 2, "col": (col + d) % 16})

    home = col // 2 == row

    @pl.when(jnp.logical_not(home))
    def _():
        greet({"row": col // 2, "col": col})

    theta_in = pltpu.make_async_copy(theta_ref, th.at[pl.ds(0, ROWS)], th_sem)
    theta_in.start()
    v_in = pltpu.make_async_copy(v_ref, vall.at[0], v_sem)
    v_in.start()

    pair_r = lax.broadcasted_iota(jnp.int32, (4, 256), 0)
    pair_c = lax.broadcasted_iota(jnp.int32, (4, 256), 1)
    second_in = (pair_r == pair_c % 4).astype(jnp.bfloat16)
    same = lax.broadcasted_iota(jnp.int32, (16, 256), 0) == lax.broadcasted_iota(jnp.int32, (16, 256), 1) // 16
    for a in range(4):
        for b in range(4):
            spread = jnp.dot(gate_ref[a, b], second_in, preferred_element_type=jnp.float32)
            spread = jnp.sum(jnp.where(pair_r == pair_c // 4 % 4, spread, 0.0), axis=0, keepdims=True)
            spread = jnp.where(same, jnp.broadcast_to(spread, (16, 256)), 0.0)
            bd[(a * 4 + b) * 16:(a * 4 + b + 1) * 16] = spread.astype(jnp.bfloat16)
    th[pl.ds(ROWS, NMAX)] = jnp.zeros((NMAX, 16, LANES), jnp.bfloat16)
    v_in.wait()
    for s in range(2):
        overlap(vall[0, s], corr_out.at[s], diag_in.at[s], 4, col)
    pl.semaphore_wait(barrier, jnp.where(home, 33, 34))

    def send_own(s, n):
        where, place = ((after, 2), (before, 3), (sibling, 1))[n]
        send(v_ref.at[s], vall.at[place, s], v_send.at[3 * s + n], v_recv.at[place, s], {"row": where, "col": col})

    for s, n in ((0, 2), (0, 0), (0, 1), (1, 2)):
        send_own(s, n)
    theta_in.wait()

    state = lax.broadcasted_iota(jnp.int32, (256, 256), 0) % 16
    state = state + 16 * (lax.broadcasted_iota(jnp.int32, (256, 256), 1) // LANES)

    def compute(u):
        place, s = ORDER[u]
        slot = places[place] * 2 + s
        if place:
            arrived(vall.at[place, s], v_recv.at[place, s])
            if place in (2, 3, 6):
                share = {2: 4, 3: 5, 6: 7}[place]
                if place == 2 and s == 0:
                    send(vall.at[2, 0], vall.at[6, 0], v_send.at[6], v_recv.at[6, 0], {"row": after, "col": col})
                if place == 3 and s == 1:
                    send(vall.at[3, 1], vall.at[6, 1], v_send.at[7], v_recv.at[6, 1], {"row": before, "col": col})
                n = 8 + 2 * (2, 3, 6).index(place) + s
                send(vall.at[place, s], vall.at[share, s], v_send.at[n], v_recv.at[share, s], {"row": sibling, "col": col})
        sector = sector_ref[slot]
        start = offset_ref[row, sector]
        end = jnp.where(sector == 15, ROWS, offset_ref[row, jnp.minimum(sector + 1, 15)])
        count = end - start
        for k in range(0, NMAX // 16, 2):
            both = th[pl.ds(start + 16 * k, 32)].reshape(512, LANES)
            both = jnp.concatenate([both[:256], both[256:]], axis=1)
            gated = jnp.dot(bd[...], both, preferred_element_type=jnp.float32)
            gated = jnp.where(state + 16 * k < count, gated, 0.0).astype(jnp.bfloat16)
            for a in range(SITES):
                for b in range(SITES):
                    for m in range(2):
                        ap[a * NMAX + 16 * (k + m): a * NMAX + 16 * (k + m + 1), b * LANES:(b + 1) * LANES] = gated[
                            (a * 4 + b) * 16:(a * 4 + b + 1) * 16, m * LANES:(m + 1) * LANES]
        product = jnp.dot(ap[...], vall[place, s], preferred_element_type=jnp.float32).astype(jnp.bfloat16)
        for a in range(SITES):
            part[u, a] = product[a * NMAX:(a + 1) * NMAX]
        axis = u % 2
        mine = z if axis == 0 else y
        far = (mine + 2) % 4
        send(part.at[u, far, pl.ds(0, HALF)], half_in.at[u, 0], half_send.at[u, 0], half_recv.at[u, 0], along(axis, 1))
        send(part.at[u, far, pl.ds(HALF, HALF)], half_in.at[u, 1], half_send.at[u, 1], half_recv.at[u, 1], along(axis, 3))

    def pass_on(u):
        axis = u % 2
        mine = z if axis == 0 else y
        for n, step in ((0, 1), (1, 3)):
            arrived(half_in.at[u, n], half_recv.at[u, n])
            to = (mine + step) % 4
            rows = pl.ds(n * HALF, HALF)
            total = part[u, to, rows, :].astype(jnp.float32) + half_in[u, n].astype(jnp.float32)
            part[u, to, rows, :] = total.astype(jnp.bfloat16)
            send(part.at[u, to], ring_in.at[u, n], ring_send.at[u, n], ring_recv.at[u, n], along(axis, step))

    def split(u):
        axis = u % 2
        mine = z if axis == 0 else y
        second = y if axis == 0 else z
        for n in range(2):
            arrived(ring_in.at[u, n], ring_recv.at[u, n])
        total = part[u, mine].astype(jnp.float32) + ring_in[u, 0].astype(jnp.float32) + ring_in[u, 1].astype(jnp.float32)
        total = total.astype(jnp.bfloat16)
        for q in range(4):
            quart[u, q] = total[:, q * LANES:(q + 1) * LANES]
        for d in (2, 1, 3):
            send(quart.at[u, (second + d) % 4], quart_in.at[u, d - 1], quart_send.at[u, d - 1],
                 quart_recv.at[u, d - 1], along(1 - axis, d))

    def finish(u):
        axis = u % 2
        place, s = ORDER[u]
        mine = z if axis == 0 else y
        second = y if axis == 0 else z
        total = quart[u, second].astype(jnp.float32)
        for d in (1, 2, 3):
            arrived(quart_in.at[u, d - 1], quart_recv.at[u, d - 1])
            total = total + quart_in[u, d - 1].astype(jnp.float32)
        done[u] = total.astype(jnp.bfloat16)
        for h in range(2):
            src = done.at[u, pl.ds(h * HALF, HALF)]
            dst = fin_ref.at[s, mine, second]
            target = 2 * row + h
            if place == 0:
                @pl.when(col == target)
                def _():
                    pltpu.make_async_copy(src, dst, fin_recv.at[s, col]).start()

                @pl.when(col != target)
                def _():
                    pltpu.make_async_remote_copy(
                        src_ref=src, dst_ref=dst, send_sem=fin_send.at[u, h], recv_sem=fin_recv.at[s, col],
                        device_id={"row": places[place], "col": target}, device_id_type=MESH).start()
            else:
                send(src, dst, fin_send.at[u, h], fin_recv.at[s, col], {"row": places[place], "col": target})

    def each(task, group):
        if 0 <= group < 4:
            for u in range(4 * group, 4 * group + 4):
                task(u)

    at_row = lax.broadcasted_iota(jnp.int32, (SHARE, KEPT), 0) + SHARE * col
    at_col = lax.broadcasted_iota(jnp.int32, (SHARE, KEPT), 1)

    def start_corr():
        for s in range(2):
            start_exchange(corr_out.at[s], corr_in.at[s], corr_send.at[s], corr_recv.at[s], row, col)

    def start_gram(s):
        @pl.loop(0, 16)
        def _(c):
            arrived(fin_ref.at[s, 0, 0], fin_recv.at[s, c])

        for a in range(SITES):
            for q in range(4):
                factor[s, a * HALF:(a + 1) * HALF, q * LANES:(q + 1) * LANES] = fin_ref[s, a, q]
        overlap(factor[s], gram_out.at[s], diag_in.at[s], 0, col)
        start_shared(diag_in.at[s], diag_send.at[s], diag_recv.at[s], row, col)
        start_exchange(gram_out.at[s], gram_in.at[s], gram_send.at[s], gram_recv.at[s], row, col)

    def refine(s):
        correlation = finish_exchange(corr_out.at[s], corr_in.at[s], corr_send.at[s], corr_recv.at[s], col)
        diags = finish_shared(diag_in.at[s], diag_send.at[s], diag_recv.at[s], col)
        corr_diag = diags[4:]
        lambdas = diags[:4] / (corr_diag + 1e-06)
        gram = finish_exchange(gram_out.at[s], gram_in.at[s], gram_send.at[s], gram_recv.at[s], col)
        kept = kept_ref[sector_ref[2 * row + s]]
        across = jnp.concatenate([lambdas[q:q + 1] for q in range(4)], axis=1)
        norms = jnp.concatenate([corr_diag[q:q + 1] for q in range(4)], axis=1)
        across = jnp.broadcast_to(across, (SHARE, KEPT))
        down = jnp.sum(jnp.where(at_row == at_col, across, 0.0), axis=1, keepdims=True)
        differ = across - down
        mean = DAMPING * (across + down)
        divisor = differ * differ + mean * mean + 1e-06
        offdiag = (gram - across * correlation) * differ / divisor
        result = jnp.where(at_row == at_col, 0.5 * (1.0 - norms), offdiag)
        result = jnp.where((at_row < kept) & (at_col < kept), result, 0.0)
        out_ref[s, col] = result.astype(jnp.bfloat16)
        start_shared(out_ref.at[s], out_send.at[s], out_recv.at[s], row, col)

    each(compute, 0)
    start_corr()
    each(pass_on, 0)
    send_own(1, 1)
    each(compute, 1)
    each(split, 0)
    send_own(1, 0)
    each(pass_on, 1)
    each(finish, 0)
    each(compute, 2)
    each(split, 1)
    each(pass_on, 2)
    each(finish, 1)
    each(split, 2)
    each(compute, 3)
    each(finish, 2)
    each(pass_on, 3)
    start_gram(0)
    each(split, 3)
    each(finish, 3)
    refine(0)
    start_gram(1)
    refine(1)
    for s in range(2):
        @pl.loop(1, 16)
        def _(d):
            source = (col + d) % 16
            wait_on(out_ref.at[s, source], out_recv.at[s, source])
            wait_on(out_ref.at[s, col], out_send.at[s, source])

    for copy in sends:
        copy.wait_send()
    for s in range(2):
        for h in range(2):
            @pl.when(col != 2 * row + h)
            def _():
                pltpu.make_async_copy(done.at[s, pl.ds(h * HALF, HALF)], done.at[s, pl.ds(h * HALF, HALF)], fin_send.at[2 * s, h]).wait()


def project(theta, gate, vectors, slot_sector, block_offsets, kept):
    bf = jnp.bfloat16
    dma = pltpu.SemaphoreType.DMA
    vmem = pl.BlockSpec(memory_space=pltpu.VMEM)
    smem = pl.BlockSpec(memory_space=pltpu.SMEM)
    hbm = pl.BlockSpec(memory_space=pl.ANY)
    return pl.pallas_call(
        project_kernel,
        out_shape=(
            jax.ShapeDtypeStruct((2, SITES, 4, HALF, LANES), bf),
            jax.ShapeDtypeStruct((2, 16, SHARE, KEPT), bf),
        ),
        in_specs=[hbm, vmem, hbm, smem, smem, smem],
        out_specs=(vmem, vmem),
        scratch_shapes=[
            pltpu.VMEM((2, 16, SHARE, KEPT), bf),
            pltpu.VMEM((2, 16, SHARE, KEPT), bf),
            pltpu.VMEM((2, SITES * HALF, KEPT), bf),
            pltpu.VMEM((2, 16, SHARE, KEPT), bf),
            pltpu.VMEM((2, 16, SHARE, KEPT), bf),
            pltpu.VMEM((2, 16, 8, LANES), jnp.float32),
            pltpu.VMEM((ROWS + NMAX, 16, LANES), bf),
            pltpu.VMEM((256, 256), bf),
            pltpu.VMEM((SITES * NMAX, KEPT), bf),
            pltpu.VMEM((8, 2, KEPT, KEPT), bf),
            pltpu.VMEM((UNITS, SITES, NMAX, KEPT), bf),
            pltpu.VMEM((UNITS, 2, HALF, KEPT), bf),
            pltpu.VMEM((UNITS, 2, NMAX, KEPT), bf),
            pltpu.VMEM((UNITS, 4, NMAX, LANES), bf),
            pltpu.VMEM((UNITS, 3, NMAX, LANES), bf),
            pltpu.VMEM((UNITS, NMAX, LANES), bf),
            dma, dma, dma((14,)), dma((8, 2)),
            dma((UNITS, 2)), dma((UNITS, 2)), dma((UNITS, 2)), dma((UNITS, 2)),
            dma((UNITS, 3)), dma((UNITS, 3)), dma((UNITS, 2)), dma((2, 16)),
        ] + [dma((2, 16))] * 8,
        compiler_params=pltpu.CompilerParams(has_side_effects=True, collective_id=0, vmem_limit_bytes=56 * 2**20),
        cost_estimate=pl.CostEstimate(flops=5_000_000_000, bytes_accessed=6_000_000, transcendentals=0),
        name="project",
    )(theta, gate, vectors, slot_sector, block_offsets, kept)


def final_kernel(sector_ref, kept_ref, v_ref, corr_ref, fin_ref, left_ref, right_ref):
    s = pl.program_id(0)
    kept = kept_ref[sector_ref[2 * lax.axis_index("row") + s]]
    corr_b = corr_ref[0].reshape(KEPT, KEPT)

    def keep(values):
        return jnp.where(lax.broadcasted_iota(jnp.int32, values.shape, 1) < kept, values, 0.0)

    for n in range(0, KEPT, 256):
        block = v_ref[0, n:n + 256]
        change = jnp.dot(block, corr_b, preferred_element_type=jnp.float32)
        right_ref[0, n:n + 256] = keep(block.astype(jnp.float32) + change)
    for a in range(SITES):
        block = jnp.concatenate([fin_ref[0, a, q] for q in range(4)], axis=1)
        change = jnp.dot(block, corr_b, preferred_element_type=jnp.float32)
        left_ref[:, 0, a, :] = keep(block.astype(jnp.float32) + change)


def final(slot_sector, kept, vectors, corr_b, fin):
    smem = pl.BlockSpec(memory_space=pltpu.SMEM)
    return pl.pallas_call(
        final_kernel,
        grid=(2,),
        out_shape=(
            jax.ShapeDtypeStruct((HALF, 2, SITES, KEPT), jnp.float32),
            jax.ShapeDtypeStruct((2, KEPT, KEPT), jnp.float32),
        ),
        in_specs=[
            smem, smem,
            pl.BlockSpec((1, KEPT, KEPT), lambda s: (s, 0, 0)),
            pl.BlockSpec((1, 16, SHARE, KEPT), lambda s: (s, 0, 0, 0)),
            pl.BlockSpec((1, SITES, 4, HALF, LANES), lambda s: (s, 0, 0, 0, 0)),
        ],
        out_specs=(
            pl.BlockSpec((HALF, 1, SITES, KEPT), lambda s: (0, s, 0, 0)),
            pl.BlockSpec((1, KEPT, KEPT), lambda s: (s, 0, 0)),
        ),
        compiler_params=pltpu.CompilerParams(vmem_limit_bytes=32 * 2**20),
        cost_estimate=pl.CostEstimate(flops=800_000_000, bytes_accessed=5_500_000, transcendentals=0),
        name="final",
    )(slot_sector, kept, vectors, corr_b, fin)


def shards(theta, gate, warm_start, slot_sector, kept, block_offsets):
    vectors = warm_start.reshape(2, KEPT, KEPT)
    fin, corr_b = project(theta.reshape(ROWS, 16, LANES), gate, vectors, slot_sector, block_offsets, kept)
    left, right = final(slot_sector, kept, vectors, corr_b, fin)
    return left, right.reshape(2, 4, LANES, KEPT)


def solution(mesh):
    in_specs = (P("row", None, None, "col"), P(), P("row", None, "col", None), P(), P(), P())
    out_specs = (P("col", "row", None, None), P("row", None, "col", None))
    return jax.shard_map(shards, mesh=mesh, in_specs=in_specs, out_specs=out_specs, check_vma=False)
```
